32 devices in a mesh: grp: 2 (over y), band: 4 (over z), sub: 2 (over x), kern: 2 (over core).
Axes of the slice: x: 2, y: 2, z: 4, core: 2. Of those that a mesh axis runs over, the one named last changes fastest.
Arguments:
- screens: bfloat16 [32, 2, 64, 64], P('band'), may hold values from -6 to 6
- visibilities: bfloat16 [1024, 2, 128], P(('grp', 'band', 'sub', 'kern')), parts along dimension 0, may hold values from -6 to 6
- vis_columns: int32 [1024, 128], P(('grp', 'band', 'sub', 'kern')), parts along dimension 0, may hold values from 0 to 63
- band_route: int32 [1024, 1], P(('grp', 'band', 'sub', 'kern')), parts along dimension 0, may hold values from 0 to 3; in each aligned block of 32 rows (0 to 31, 32 to 63, ...) at most 16 rows name the same one
- screen_choice: int32 [1024], P(('grp', 'band', 'sub', 'kern')), parts along dimension 0, may hold values from 0 to 31
- offsets: int32 [1024, 2], P(('grp', 'band', 'sub', 'kern')), parts along dimension 0, may hold values from 0 to 7
- row_cell: int32 [1024], P(('grp', 'band', 'sub', 'kern')), parts along dimension 0, may hold values from 0 to 192
- col_cell: int32 [1024], P(('grp', 'band', 'sub', 'kern')), parts along dimension 0, may hold values from 0 to 896
Outputs:
- grid: float32 [2, 2048, 1024], P(None, ('grp', 'band', 'sub', 'kern')), parts along dimension 1
The draws below stay inside these ranges and needn't reach their ends.
There are 2 independent parts, one for each index of `grp`. The reference program is written for one: setup_inputs(seed, part) draws one part's arguments, and reference() takes and returns one part's arrays. A program takes and returns all parts, laid end to end along the dimension named above; an argument that names none is the same for every part. Nothing has to cross between parts.
Inputs may be any that keep to these rules, and one draw needn't show every extreme that they name: `band_route`: among the blocks of one device no band is named more than 16 times, a bound that some block reaches.
All inputs are finite; a program needn't handle non-finite values.
Results may differ from the reference program's by a relative error of at most 0.0058.
Values may be sent and summed in bfloat16 or wider, within the bound.
A program may use at most 64 MiB of HBM per device.

```python
import math
import jax
import jax.numpy as jnp
import numpy as np
from jax import lax

KS = 64
OVERS = 8
VB = 128
BR = 256
NCOL = 1024
NB_DEV = 32
NK = 32
CAP = 16
NBLK = 512
NROW = 1024
N_BAND = 4


def touch_ends(result, own_key, smallest, top_value):
    spot = [jax.random.randint(jax.random.fold_in(own_key, axis), (), 0, length) for axis, length in enumerate(result.shape)]
    longest = result.shape.index(max(result.shape))
    beside = spot[:longest] + [(spot[longest] + 1) % result.shape[longest]] + spot[longest + 1:]
    return result.at[tuple(spot)].set(smallest).at[tuple(beside)].set(top_value)


def steps_of(own_key, extent, shards, smallest, high):
    level = 1.0
    for axis_at, blocks in shards:
        heights = jax.random.uniform(jax.random.fold_in(jax.random.fold_in(own_key, 6), axis_at), (blocks,), jnp.float32, smallest / len(shards), high / len(shards))
        level = level * jnp.repeat(jnp.exp(heights), extent[axis_at] // blocks).reshape((-1,) + (1,) * (len(extent) - 1 - axis_at))
    return level


def assign_block(stream_key, own, number, rows, number_of, top, limit, lean):
    order = jax.random.permutation(stream_key, number_of)
    packed, ordinary = shares(number_of, rows * top, limit, lean, True), shares(number_of, rows * top, limit, lean, False)
    places = jnp.arange(number_of)

    def named(lengths, offset_by):
        used = int((lengths > 0).sum())
        fixed = max(1, used // 4)
        passed = fixed + (places - fixed + offset_by * (used - fixed)) % max(1, number_of - fixed)
        return jnp.zeros((number_of,), jnp.int32).at[order[jnp.where(places < fixed, places, passed)]].set(jnp.asarray(lengths, jnp.int32))

    lengths = jnp.where(number % 4 == 0, named(packed, number // 4), named(ordinary, number - number // 4 - 1))
    mixed = jax.random.permutation(jax.random.fold_in(own, 3), number_of)
    giver, taker = mixed[0:number_of // 2 * 2:2], mixed[1:number_of // 2 * 2:2]
    margin = jnp.minimum(lengths[giver] - 1, limit - lengths[taker]) // 2
    margin = jnp.where((giver == order[0]) | (taker == order[0]) | (lengths[taker] == 0), 0, jnp.maximum(margin, 0))
    passed = jax.random.randint(jax.random.fold_in(own, 4), (number_of // 2,), 0, 1 << 20) % (margin + 1)
    lengths = lengths.at[giver].add(-passed).at[taker].add(passed)
    labels = jnp.searchsorted(jnp.cumsum(lengths), jnp.arange(rows * top), side="right").astype(jnp.int32)
    table = labels.reshape(top, rows).T
    table = table[jax.random.permutation(jax.random.fold_in(own, 1), rows)]
    offset_by = jax.random.randint(jax.random.fold_in(own, 2), (rows, 1), 0, top)
    return jnp.take_along_axis(table, (jnp.arange(top)[None, :] + offset_by) % top, axis=1)


def shares(number_of, total, most, slope, full):
    loads = [(1 << 20) // math.isqrt(rank ** slope) + 1 for rank in range(1, number_of + 1)]
    largest = most if full else min(most, max(-(-total // number_of), total * loads[0] // sum(loads)))
    least = 1 if total - largest >= number_of - 1 else 0
    counts, spare = [largest] + [least] * (number_of - 1), total - largest - least * (number_of - 1)
    while spare > 0:
        candidates = [i for i in range(1, number_of) if counts[i] < largest] or [i for i in range(1, number_of) if counts[i] < most]
        pool, budget = sum([loads[i] for i in candidates]), spare
        for i in candidates:
            extra = min(most - counts[i], max(1, budget * loads[i] // pool), spare)
            counts[i] = counts[i] + extra
            spare = spare - extra
    return np.array(counts)


def bell_draw(key, shape, spread, bound, split=(), held_as=jnp.bfloat16):
    level = steps_of(key, shape, split, -0.22, 0.18) if split else 1.0
    values = jax.random.normal(key, shape, jnp.float32) * spread * level
    return jnp.minimum(jnp.maximum(values, -bound), bound).astype(held_as)


def setup_inputs(seed: int = 0, part: int = 0) -> dict:
    arg_keys = jax.random.split(jax.random.key(seed), 9)
    part_splits = jax.random.split(jax.random.fold_in(arg_keys[8], part), 9)
    screens = bell_draw(arg_keys[0], (NK, 2, KS, KS), 1.0, 6.0, ((0, 4),))
    visibilities = bell_draw(part_splits[1], (NBLK, 2, VB), 1.0, 6.0, ((0, 16),))
    vis_columns = touch_ends(jax.random.randint(part_splits[2], (NBLK, VB), 0, KS), jax.random.fold_in(part_splits[2], 1), 0, KS - 1).astype(jnp.int32)
    band_route_keys = jax.random.split(jax.random.fold_in(part_splits[3], 1), NBLK // NB_DEV)
    band_route_turns = jax.random.permutation(jax.random.fold_in(part_splits[3], 3), NBLK // NB_DEV)
    band_route = jax.vmap(lambda own, number: assign_block(jax.random.fold_in(part_splits[3], 2), own, number, NB_DEV, N_BAND, 1, CAP, 2))(band_route_keys, band_route_turns).reshape((NBLK, 1))
    screen_choice = touch_ends(jax.random.randint(part_splits[4], (NBLK,), 0, NK), jax.random.fold_in(part_splits[4], 1), 0, NK - 1).astype(jnp.int32)
    offsets = touch_ends(jax.random.randint(part_splits[5], (NBLK, 2), 0, OVERS), jax.random.fold_in(part_splits[5], 1), 0, OVERS - 1).astype(jnp.int32)
    row_cell = touch_ends(jax.random.randint(part_splits[6], (NBLK,), 0, BR - KS + 1), jax.random.fold_in(part_splits[6], 1), 0, BR - KS).astype(jnp.int32)
    col_cell = touch_ends(jax.random.randint(part_splits[7], (NBLK,), 0, NCOL - 2 * KS + 1), jax.random.fold_in(part_splits[7], 1), 0, NCOL - 2 * KS).astype(jnp.int32)
    return {"screens": screens, "visibilities": visibilities, "vis_columns": vis_columns, "band_route": band_route, "screen_choice": screen_choice, "offsets": offsets, "row_cell": row_cell, "col_cell": col_cell}


ref_group = 16


def settle(array_in):
    return lax.optimization_barrier(array_in.astype(jnp.bfloat16)).astype(jnp.float32)


def dft_tables(support):
    centred = jnp.arange(support, dtype=jnp.float32) - support // 2
    fractions = jnp.arange(OVERS, dtype=jnp.float32) / OVERS
    frequency = centred[None, :, None] + fractions[:, None, None]
    phases = -2.0 * math.pi * frequency * centred[None, None, :] / support
    return settle(jnp.stack([jnp.cos(phases), jnp.sin(phases)], axis=1) / support)


def complex_product(left_side, right_side, pattern):
    left_side = left_side.astype(jnp.float32)
    right_side = right_side.astype(jnp.float32)
    left_real, left_imag = left_side[:, 0], left_side[:, 1]
    right_real, right_imag = right_side[:, 0], right_side[:, 1]
    real_part = jnp.einsum(pattern, left_real, right_real) - jnp.einsum(pattern, left_imag, right_imag)
    imag_part = jnp.einsum(pattern, left_real, right_imag) + jnp.einsum(pattern, left_imag, right_real)
    return jnp.stack([real_part, imag_part], axis=1)


def build_kernels(tables, chosen, row_off, col_off):
    row_table = jnp.take(tables, row_off, axis=0)
    col_table = jnp.take(tables, col_off, axis=0)
    half_dft = settle(complex_product(row_table, chosen, "bum,bml->bul"))
    return settle(complex_product(half_dft, col_table, "bul,bvl->buv"))


def block_patches(kernels, values, columns):
    support = kernels.shape[-1]
    patch_width = 2 * support
    count = kernels.shape[0]
    onehot = (columns[:, :, None] == jnp.arange(support, dtype=jnp.int32)[None, None, :]).astype(jnp.float32)
    column_line = settle(jnp.einsum("bzv,bvc->bzc", values.astype(jnp.float32), onehot))
    padded = jnp.pad(column_line, ((0, 0), (0, 0), (0, patch_width + 1 - support)))
    toeplitz = jnp.tile(padded, (1, 1, support))[:, :, :support * patch_width]
    toeplitz = toeplitz.reshape(count, 2, support, patch_width)
    return complex_product(kernels, toeplitz, "bxj,bjy->bxy")


def add_patches(grid_band, patches, rows_at, cols_at):
    for index_slot in range(patches.shape[0]):
        corner = (jnp.int32(0), rows_at[index_slot], cols_at[index_slot])
        current = lax.dynamic_slice(grid_band, corner, patches.shape[1:])
        grid_band = lax.dynamic_update_slice(grid_band, current + patches[index_slot], corner)
    return grid_band


def reference(screens, visibilities, vis_columns, band_route, screen_choice, offsets, row_cell, col_cell):
    tables = dft_tables(KS)
    global_rows = (band_route[:, 0] * BR + row_cell).astype(jnp.int32)
    grid_full = jnp.zeros((2, NROW, NCOL), jnp.float32)

    def grid_turn(group_index, grid_full):
        first = (group_index * ref_group).astype(jnp.int32)

        def take_group(source):
            return lax.dynamic_slice_in_dim(source, first, ref_group, 0)

        group_offsets = take_group(offsets)
        chosen = jnp.take(screens, take_group(screen_choice), axis=0)
        kernels = build_kernels(tables, chosen, group_offsets[:, 0], group_offsets[:, 1])
        patches = block_patches(kernels, take_group(visibilities), take_group(vis_columns))
        return add_patches(grid_full, patches, take_group(global_rows), take_group(col_cell))

    return lax.fori_loop(0, NBLK // ref_group, grid_turn, grid_full)
```

```python
import functools
import math

import jax
import jax.numpy as jnp
import numpy as np
from jax import lax
from jax.experimental import pallas as pl
from jax.experimental.pallas import tpu as pltpu
from jax.sharding import PartitionSpec as P

OVERS = 8
BR = 256
NCOL = 1024
SUBLANES = 8
GROUP = 4


def dft_tables(support):
    centred = np.arange(support, dtype=np.float32) - np.float32(support // 2)
    fractions = np.arange(OVERS, dtype=np.float32) / np.float32(OVERS)
    frequency = centred[None, :, None] + fractions[:, None, None]
    phases = np.float32(-2.0 * math.pi) * frequency * centred[None, None, :] / np.float32(support)
    tables = np.stack([np.cos(phases), np.sin(phases)], axis=1) / np.float32(support)
    return tables.astype(jnp.bfloat16).astype(np.float32)


def row_tables(tables, patch_rows):
    support = tables.shape[-1]
    shifted = np.zeros((OVERS, SUBLANES + 1, patch_rows, 2 * support), np.float32)
    wide = np.concatenate([tables[:, 0], tables[:, 1]], axis=-1)
    for shift in range(SUBLANES + 1):
        shifted[:, shift, shift : shift + support] = wide
    return jnp.asarray(shifted.reshape(-1, patch_rows, 2 * support), jnp.bfloat16)


def col_tables(tables):
    real, imag = tables[:, 0].swapaxes(1, 2), tables[:, 1].swapaxes(1, 2)
    upper = np.concatenate([real, imag], axis=-1)
    lower = np.concatenate([-imag, real], axis=-1)
    return jnp.asarray(np.concatenate([upper, lower], axis=1), jnp.bfloat16)


def grid_kernel(support, meta, screens, lines, rows_tab, cols_tab, grid, hats, picked):
    width = 2 * support
    window = support + SUBLANES
    blocks = meta.shape[1]
    me = lax.axis_index("band")
    lane = lax.broadcasted_iota(jnp.int32, (support, width), 1)

    def make_hat(s, carry):
        upper = screens[s].astype(jnp.float32)
        turned = pltpu.roll(upper, support, 1)
        lower = jnp.where(lane < support, -turned, turned)
        hats[s, 0:support, :] = upper.astype(jnp.bfloat16)
        hats[s, support:width, :] = lower.astype(jnp.bfloat16)
        return carry

    lax.fori_loop(0, screens.shape[0], make_hat, 0)
    grid[...] = jnp.zeros_like(grid)

    def pick(i, count):
        picked[count] = i
        return count + (meta[0, i] == me).astype(jnp.int32)

    count = lax.fori_loop(0, blocks, pick, jnp.int32(0))
    for k in range(GROUP):
        picked[count + k] = 0
    lane_window = lax.broadcasted_iota(jnp.int32, (window, width), 1)

    def turn(g, carry):
        patches = []
        for k in range(GROUP):
            slot = g * GROUP + k
            i = picked[slot]
            keep = (slot < count).astype(jnp.float32)
            row, col = meta[4, i], meta[5, i]
            row_at = jnp.minimum(row // SUBLANES, (BR - window) // SUBLANES)
            col_at = jnp.minimum(col // width, NCOL // width - 2)
            row_shift = row - row_at * SUBLANES
            col_shift = col - col_at * width
            half = jnp.dot(
                rows_tab[meta[2, i] * (SUBLANES + 1) + row_shift],
                hats[meta[1, i]],
                preferred_element_type=jnp.float32,
            ).astype(jnp.bfloat16)
            kernel = jnp.dot(
                half, cols_tab[meta[3, i]], preferred_element_type=jnp.float32
            ).astype(jnp.bfloat16)
            line = lines[i] * keep
            spread = [
                pltpu.roll(
                    jnp.broadcast_to(line[z : z + 1, :], (support, width)),
                    0,
                    1,
                    stride=1,
                    stride_axis=0,
                )
                for z in range(2)
            ]
            toeplitz = jnp.concatenate(
                [
                    jnp.concatenate([spread[0], spread[1]], axis=1),
                    jnp.concatenate([-spread[1], spread[0]], axis=1),
                ],
                axis=0,
            ).astype(jnp.bfloat16)
            patch = jnp.dot(kernel, toeplitz, preferred_element_type=jnp.float32)
            patches.append((patch, row_at, col_at, col_shift))
        for patch, row_at, col_at, col_shift in patches:
            rows = pl.ds(pl.multiple_of(row_at * SUBLANES, SUBLANES), window)
            left = pl.ds(pl.multiple_of(col_at * width, width), width)
            right = pl.ds(pl.multiple_of(col_at * width + width, width), width)
            for z in range(2):
                turned = pltpu.roll(
                    patch[:window, z * width : (z + 1) * width], lax.rem(col_shift, width), 1
                )
                inside = lane_window >= col_shift
                grid[z, rows, left] += jnp.where(inside, turned, 0.0)
                grid[z, rows, right] += jnp.where(inside, 0.0, turned)
        return carry

    lax.fori_loop(0, (count + GROUP - 1) // GROUP, turn, 0)


def make_lines(visibilities, vis_columns, support):
    onehot = (
        vis_columns[:, :, None] == jnp.arange(2 * support, dtype=jnp.int32)[None, None, :]
    ).astype(jnp.bfloat16)
    return jnp.einsum(
        "bzv,bvc->bzc", visibilities, onehot, preferred_element_type=jnp.float32
    ).astype(jnp.bfloat16)


def body(
    screens, visibilities, vis_columns, band_route, screen_choice, offsets, row_cell, col_cell
):
    support = screens.shape[-1]
    width = 2 * support
    tables = dft_tables(support)
    patch_rows = -(-(support + SUBLANES) // 16) * 16
    wide = jnp.concatenate([screens[:, 0], screens[:, 1]], axis=-1)
    meta = jnp.stack(
        [band_route[:, 0], screen_choice, offsets[:, 0], offsets[:, 1], row_cell, col_cell]
    )
    lines = make_lines(visibilities, vis_columns, support)
    every_screen = lax.all_gather(wide, "band", axis=0, tiled=True)
    every_line = lax.all_gather(lines, "band", axis=0, tiled=True).astype(jnp.float32)
    every_meta = lax.all_gather(meta, "band", axis=1, tiled=True)
    vmem = pl.BlockSpec(memory_space=pltpu.VMEM)
    grid_band = pl.pallas_call(
        functools.partial(grid_kernel, support),
        out_shape=jax.ShapeDtypeStruct((2, BR, NCOL), jnp.float32),
        in_specs=[pl.BlockSpec(memory_space=pltpu.SMEM), vmem, vmem, vmem, vmem],
        out_specs=vmem,
        scratch_shapes=[
            pltpu.VMEM((every_screen.shape[0], width, width), jnp.bfloat16),
            pltpu.SMEM((every_meta.shape[1] + GROUP,), jnp.int32),
        ],
        compiler_params=pltpu.CompilerParams(vmem_limit_bytes=32 * 1024 * 1024),
    )(every_meta, every_screen, every_line, row_tables(tables, patch_rows), col_tables(tables))
    return lax.psum_scatter(grid_band, ("sub", "kern"), scatter_dimension=1, tiled=True)


def solution(mesh):
    in_specs = (
        P("band", None, None, None),
        P(("grp", "band", "sub", "kern"), None, None),
        P(("grp", "band", "sub", "kern"), None),
        P(("grp", "band", "sub", "kern"), None),
        P(("grp", "band", "sub", "kern")),
        P(("grp", "band", "sub", "kern"), None),
        P(("grp", "band", "sub", "kern")),
        P(("grp", "band", "sub", "kern")),
    )
    out_specs = P(None, ("grp", "band", "sub", "kern"), None)
    return jax.shard_map(body, mesh=mesh, in_specs=in_specs, out_specs=out_specs, check_vma=False)
```

```python
import functools
import math

import jax
import jax.numpy as jnp
import numpy as np
from jax import lax
from jax.experimental import pallas as pl
from jax.experimental.pallas import tpu as pltpu
from jax.sharding import PartitionSpec as P

OVERS = 8
BR = 256
NCOL = 1024
SUBLANES = 8
GROUP = 4
SUM_PARTS = 2
MESH = pl.DeviceIdType.MESH


def dft_tables(support):
    centred = np.arange(support, dtype=np.float32) - np.float32(support // 2)
    fractions = np.arange(OVERS, dtype=np.float32) / np.float32(OVERS)
    frequency = centred[None, :, None] + fractions[:, None, None]
    phases = np.float32(-2.0 * math.pi) * frequency * centred[None, None, :] / np.float32(support)
    tables = np.stack([np.cos(phases), np.sin(phases)], axis=1) / np.float32(support)
    return tables.astype(jnp.bfloat16).astype(np.float32)


def row_tables(tables, patch_rows):
    support = tables.shape[-1]
    shifted = np.zeros((OVERS, SUBLANES + 1, patch_rows, 2 * support), np.float32)
    wide = np.concatenate([tables[:, 0], tables[:, 1]], axis=-1)
    for shift in range(SUBLANES + 1):
        shifted[:, shift, shift : shift + support] = wide
    return jnp.asarray(shifted.reshape(-1, patch_rows, 2 * support), jnp.bfloat16)


def col_tables(tables):
    real, imag = tables[:, 0].swapaxes(1, 2), tables[:, 1].swapaxes(1, 2)
    upper = np.concatenate([real, imag], axis=-1)
    lower = np.concatenate([-imag, real], axis=-1)
    return jnp.asarray(np.concatenate([upper, lower], axis=1), jnp.bfloat16)


def gather_kernel(band_count, sub_count, kern_count, refs_in, refs_out, sems):
    screens, lines, meta = refs_in
    every_screen, every_line, every_meta = refs_out
    far_send, far_recv, mate_send, mate_recv, own_sem = sems
    own = screens.shape[0]
    line_rows = lines.shape[0]
    band, sub, kern = (lax.axis_index(name) for name in ("band", "sub", "kern"))
    if screens.shape[1] % (16 * sub_count * kern_count):
        fan_count, fan = 1, 0
    else:
        fan_count, fan = sub_count, sub
    part = screens.shape[1] // (fan_count * kern_count)
    mine = pl.ds((fan * kern_count + kern) * part, part)
    peers = [lax.rem(band + d, band_count) for d in range(1, band_count)]
    mates = [
        (lax.rem(sub + s, sub_count), lax.rem(kern + k, kern_count))
        for s in range(fan_count)
        for k in range(kern_count)
        if s or k
    ]
    barrier = pltpu.get_barrier_semaphore()
    for peer in peers:
        pl.semaphore_signal(barrier, inc=1, device_id={"band": peer}, device_id_type=MESH)
    for mate in mates:
        pl.semaphore_signal(
            barrier, inc=1, device_id={"sub": mate[0], "kern": mate[1]}, device_id_type=MESH
        )
    pl.semaphore_wait(barrier, len(peers) + len(mates))

    here_screen = every_screen.at[pl.ds(band * own, own)]
    here_line = every_line.at[pl.ds(band * line_rows, line_rows)]
    here_meta = every_meta.at[pl.ds(band, 1)]
    far = []
    for n, peer in enumerate(peers):
        for a, (source, target) in enumerate(
            [
                (screens.at[:, mine], here_screen.at[:, mine]),
                (lines, here_line),
                (meta, here_meta),
            ]
        ):
            copy = pltpu.make_async_remote_copy(
                src_ref=source,
                dst_ref=target,
                send_sem=far_send.at[n, a],
                recv_sem=far_recv.at[n, a],
                device_id={"band": peer},
                device_id_type=MESH,
            )
            copy.start()
            far.append(copy)
    own_copies = [
        pltpu.make_async_copy(source, target, own_sem.at[a])
        for a, (source, target) in enumerate(
            [(screens, here_screen), (lines, here_line), (meta, here_meta)]
        )
    ]
    for copy in own_copies:
        copy.start()
    near = []
    for n in range(len(peers)):
        source_band = lax.rem(band + band_count - 1 - n, band_count)
        piece = every_screen.at[pl.ds(source_band * own, own), mine]
        far[3 * n].wait_recv()
        for m, mate in enumerate(mates):
            copy = pltpu.make_async_remote_copy(
                src_ref=piece,
                dst_ref=piece,
                send_sem=mate_send.at[n, m],
                recv_sem=mate_recv.at[n, m],
                device_id={"sub": mate[0], "kern": mate[1]},
                device_id_type=MESH,
            )
            copy.start()
            near.append(copy)
    for n in range(len(peers)):
        far[3 * n + 1].wait_recv()
        far[3 * n + 2].wait_recv()
    for copy in own_copies:
        copy.wait()
    for copy in near:
        copy.wait()
    for copy in far:
        copy.wait_send()


def gather(wide, lines, meta):
    band_count, sub_count, kern_count = (lax.axis_size(name) for name in ("band", "sub", "kern"))
    peers, mates = max(band_count - 1, 1), max(sub_count * kern_count - 1, 1)

    def kernel(*refs):
        gather_kernel(band_count, sub_count, kern_count, refs[:3], refs[3:6], refs[6:])

    vmem = pl.BlockSpec(memory_space=pltpu.VMEM)
    dma = pltpu.SemaphoreType.DMA
    return pl.pallas_call(
        kernel,
        out_shape=[
            jax.ShapeDtypeStruct((band_count * x.shape[0],) + x.shape[1:], x.dtype)
            for x in (wide, lines, meta)
        ],
        in_specs=[vmem] * 3,
        out_specs=[vmem] * 3,
        scratch_shapes=[
            dma((peers, 3)),
            dma((peers, 3)),
            dma((peers, mates)),
            dma((peers, mates)),
            dma((3,)),
        ],
        compiler_params=pltpu.CompilerParams(
            collective_id=0, has_side_effects=True, vmem_limit_bytes=32 * 1024 * 1024
        ),
    )(wide, lines, meta)


def sum_kernel(sub_count, kern_count, grid, out, core_out, core_in, far_out, far_in, sems):
    core_send, core_recv, far_send, far_recv = sems
    rows = out.shape[1]
    step = rows // SUM_PARTS
    sub, kern = lax.axis_index("sub"), lax.axis_index("kern")
    cores = [lax.rem(kern + k, kern_count) for k in range(1, kern_count)]
    subs = [lax.rem(sub + s, sub_count) for s in range(1, sub_count)]
    barrier = pltpu.get_barrier_semaphore()
    for core in cores:
        pl.semaphore_signal(barrier, inc=1, device_id={"kern": core}, device_id_type=MESH)
    for other in subs:
        pl.semaphore_signal(barrier, inc=1, device_id={"sub": other}, device_id_type=MESH)
    pl.semaphore_wait(barrier, len(cores) + len(subs))

    def rows_of(owner_sub, owner_kern, part):
        start = (owner_sub * kern_count + owner_kern) * rows + part * step
        return pl.ds(pl.multiple_of(start, step), step)

    parts = [(z, p) for z in range(2) for p in range(SUM_PARTS)]
    order = [(s, owner) for s, owner in enumerate(subs)] + [(len(subs), sub)]
    near, far = {}, {}
    for s, owner in order:
        for z, p in parts:
            for k, core in enumerate(cores):
                spot = (s, k, z, pl.ds(p * step, step))
                core_out[spot] = grid[z, rows_of(owner, core, p)].astype(jnp.bfloat16)
                copy = pltpu.make_async_remote_copy(
                    src_ref=core_out.at[spot],
                    dst_ref=core_in.at[spot],
                    send_sem=core_send.at[s, k, z, p],
                    recv_sem=core_recv.at[s, k, z, p],
                    device_id={"kern": core},
                    device_id_type=MESH,
                )
                copy.start()
                near[s, k, z, p] = copy

    def chip_total(s, owner, z, p):
        total = grid[z, rows_of(owner, kern, p)]
        for k in range(len(cores)):
            near[s, k, z, p].wait_recv()
            total += core_in[s, k, z, pl.ds(p * step, step)].astype(jnp.float32)
        return total

    for s, owner in order[:-1]:
        for z, p in parts:
            spot = (s, z, pl.ds(p * step, step))
            far_out[spot] = chip_total(s, owner, z, p).astype(jnp.bfloat16)
            copy = pltpu.make_async_remote_copy(
                src_ref=far_out.at[spot],
                dst_ref=far_in.at[spot],
                send_sem=far_send.at[s, z, p],
                recv_sem=far_recv.at[s, z, p],
                device_id={"sub": owner},
                device_id_type=MESH,
            )
            copy.start()
            far[s, z, p] = copy
    for z, p in parts:
        out[z, pl.ds(p * step, step)] = chip_total(len(subs), sub, z, p)
    for z, p in parts:
        for s in range(len(subs)):
            far[s, z, p].wait_recv()
            out[z, pl.ds(p * step, step)] += far_in[s, z, pl.ds(p * step, step)].astype(
                jnp.float32
            )
    for copy in [*near.values(), *far.values()]:
        copy.wait_send()


def sum_rows(grid):
    sub_count, kern_count = lax.axis_size("sub"), lax.axis_size("kern")
    rows = grid.shape[1] // (sub_count * kern_count)
    subs, cores = max(sub_count - 1, 1), max(kern_count - 1, 1)

    def kernel(*refs):
        sum_kernel(sub_count, kern_count, *refs[:6], refs[6:])

    vmem = pl.BlockSpec(memory_space=pltpu.VMEM)
    dma = pltpu.SemaphoreType.DMA
    part = (2, rows, grid.shape[2])
    return pl.pallas_call(
        kernel,
        out_shape=jax.ShapeDtypeStruct(part, jnp.float32),
        in_specs=[vmem],
        out_specs=vmem,
        scratch_shapes=[
            pltpu.VMEM((sub_count, cores) + part, jnp.bfloat16),
            pltpu.VMEM((sub_count, cores) + part, jnp.bfloat16),
            pltpu.VMEM((subs,) + part, jnp.bfloat16),
            pltpu.VMEM((subs,) + part, jnp.bfloat16),
            dma((sub_count, cores, 2, SUM_PARTS)),
            dma((sub_count, cores, 2, SUM_PARTS)),
            dma((subs, 2, SUM_PARTS)),
            dma((subs, 2, SUM_PARTS)),
        ],
        compiler_params=pltpu.CompilerParams(
            collective_id=1, has_side_effects=True, vmem_limit_bytes=32 * 1024 * 1024
        ),
    )(grid)


def grid_kernel(
    support, blocks, meta, screens, lines, rows_tab, cols_tab, grid, hats, line_rows, picked
):
    width = 2 * support
    window = support + SUBLANES
    sources = meta.shape[0]
    me = lax.axis_index("band")
    lane = lax.broadcasted_iota(jnp.int32, (support, width), 1)

    def make_hat(s, carry):
        upper = screens[s].astype(jnp.float32)
        turned = pltpu.roll(upper, support, 1)
        lower = jnp.where(lane < support, -turned, turned)
        hats[s, 0:support, :] = upper.astype(jnp.bfloat16)
        hats[s, support:width, :] = lower.astype(jnp.bfloat16)
        return carry

    lax.fori_loop(0, screens.shape[0], make_hat, 0, unroll=8)
    grid[...] = jnp.zeros_like(grid)
    line_rows[...] = lines[...].astype(jnp.float32)

    def pick_source(source, count):
        for b in range(blocks):
            picked[count] = source * blocks + b
            count = count + (meta[source, 0, b] == me).astype(jnp.int32)
        return count

    count = lax.fori_loop(0, sources, pick_source, jnp.int32(0))
    for k in range(GROUP):
        picked[count + k] = 0
    lane_window = lax.broadcasted_iota(jnp.int32, (window, width), 1)

    def turn(g, carry):
        patches = []
        for k in range(GROUP):
            slot = g * GROUP + k
            i = picked[slot]
            source, b = lax.div(i, blocks), lax.rem(i, blocks)
            screen, row_off, col_off, row, col = (meta[source, f, b] for f in range(1, 6))
            keep = (slot < count).astype(jnp.float32)
            row_at = jnp.minimum(row // SUBLANES, (BR - window) // SUBLANES)
            col_at = jnp.minimum(col // width, NCOL // width - 2)
            row_shift = row - row_at * SUBLANES
            col_shift = col - col_at * width
            half = jnp.dot(
                rows_tab[row_off * (SUBLANES + 1) + row_shift],
                hats[screen],
                preferred_element_type=jnp.float32,
            ).astype(jnp.bfloat16)
            kernel = jnp.dot(
                half, cols_tab[col_off], preferred_element_type=jnp.float32
            ).astype(jnp.bfloat16)
            spread = [
                pltpu.roll(
                    jnp.broadcast_to(
                        line_rows[pl.ds(2 * i + z, 1), :] * keep, (support, width)
                    ),
                    0,
                    1,
                    stride=1,
                    stride_axis=0,
                )
                for z in range(2)
            ]
            toeplitz = jnp.concatenate(
                [
                    jnp.concatenate([spread[0], spread[1]], axis=1),
                    jnp.concatenate([-spread[1], spread[0]], axis=1),
                ],
                axis=0,
            ).astype(jnp.bfloat16)
            patch = jnp.dot(kernel, toeplitz, preferred_element_type=jnp.float32)
            patches.append((patch, row_at, col_at, col_shift))
        for patch, row_at, col_at, col_shift in patches:
            rows = pl.ds(pl.multiple_of(row_at * SUBLANES, SUBLANES), window)
            left = pl.ds(pl.multiple_of(col_at * width, width), width)
            right = pl.ds(pl.multiple_of(col_at * width + width, width), width)
            for z in range(2):
                turned = pltpu.roll(
                    patch[:window, z * width : (z + 1) * width], lax.rem(col_shift, width), 1
                )
                inside = lane_window >= col_shift
                grid[z, rows, left] += jnp.where(inside, turned, 0.0)
                grid[z, rows, right] += jnp.where(inside, 0.0, turned)
        return carry

    lax.fori_loop(0, (count + GROUP - 1) // GROUP, turn, 0)


def make_lines(visibilities, vis_columns, support):
    onehot = (
        vis_columns[:, :, None] == jnp.arange(2 * support, dtype=jnp.int32)[None, None, :]
    ).astype(jnp.bfloat16)
    return jnp.einsum(
        "bzv,bvc->bzc", visibilities, onehot, preferred_element_type=jnp.float32
    ).astype(jnp.bfloat16)


def body(
    screens, visibilities, vis_columns, band_route, screen_choice, offsets, row_cell, col_cell
):
    support = screens.shape[-1]
    width = 2 * support
    tables = dft_tables(support)
    patch_rows = -(-(support + SUBLANES) // 16) * 16
    wide = jnp.concatenate([screens[:, 0], screens[:, 1]], axis=-1)
    meta = jnp.stack(
        [band_route[:, 0], screen_choice, offsets[:, 0], offsets[:, 1], row_cell, col_cell]
    )
    lines = make_lines(visibilities, vis_columns, support)
    lines = lines.reshape(-1, width)
    blocks = meta.shape[1]
    meta = jnp.pad(meta, ((0, SUBLANES - meta.shape[0]), (0, -blocks % 128)))[None]
    every_screen, every_line, every_meta = gather(wide, lines, meta)
    vmem = pl.BlockSpec(memory_space=pltpu.VMEM)
    grid_band = pl.pallas_call(
        functools.partial(grid_kernel, support, blocks),
        out_shape=jax.ShapeDtypeStruct((2, BR, NCOL), jnp.float32),
        in_specs=[pl.BlockSpec(memory_space=pltpu.SMEM), vmem, vmem, vmem, vmem],
        out_specs=vmem,
        scratch_shapes=[
            pltpu.VMEM((every_screen.shape[0], width, width), jnp.bfloat16),
            pltpu.VMEM(every_line.shape, jnp.float32),
            pltpu.SMEM((every_meta.shape[0] * blocks + GROUP,), jnp.int32),
        ],
        compiler_params=pltpu.CompilerParams(vmem_limit_bytes=32 * 1024 * 1024),
    )(every_meta, every_screen, every_line, row_tables(tables, patch_rows), col_tables(tables))
    return sum_rows(grid_band)


def solution(mesh):
    in_specs = (
        P("band", None, None, None),
        P(("grp", "band", "sub", "kern"), None, None),
        P(("grp", "band", "sub", "kern"), None),
        P(("grp", "band", "sub", "kern"), None),
        P(("grp", "band", "sub", "kern")),
        P(("grp", "band", "sub", "kern"), None),
        P(("grp", "band", "sub", "kern")),
        P(("grp", "band", "sub", "kern")),
    )
    out_specs = P(None, ("grp", "band", "sub", "kern"), None)
    return jax.shard_map(body, mesh=mesh, in_specs=in_specs, out_specs=out_specs, check_vma=False)
```

```python
import functools
import math

import jax
import jax.numpy as jnp
import numpy as np
from jax import lax
from jax.experimental import pallas as pl
from jax.experimental.pallas import tpu as pltpu
from jax.sharding import PartitionSpec as P

OVERS = 8
BR = 256
NCOL = 1024
SUBLANES = 8
GROUP = 8
SUM_PARTS = 2
MESH = pl.DeviceIdType.MESH


def dft_tables(support):
    centred = np.arange(support, dtype=np.float32) - np.float32(support // 2)
    fractions = np.arange(OVERS, dtype=np.float32) / np.float32(OVERS)
    frequency = centred[None, :, None] + fractions[:, None, None]
    phases = np.float32(-2.0 * math.pi) * frequency * centred[None, None, :] / np.float32(support)
    tables = np.stack([np.cos(phases), np.sin(phases)], axis=1) / np.float32(support)
    return tables.astype(jnp.bfloat16).astype(np.float32)


def row_tables(tables, patch_rows):
    support = tables.shape[-1]
    shifted = np.zeros((OVERS, SUBLANES + 1, patch_rows, 2 * support), np.float32)
    wide = np.concatenate([tables[:, 0], tables[:, 1]], axis=-1)
    for shift in range(SUBLANES + 1):
        shifted[:, shift, shift : shift + support] = wide
    return jnp.asarray(shifted.reshape(-1, patch_rows, 2 * support), jnp.bfloat16)


def col_tables(tables):
    real, imag = tables[:, 0].swapaxes(1, 2), tables[:, 1].swapaxes(1, 2)
    upper = np.concatenate([real, imag], axis=-1)
    lower = np.concatenate([-imag, real], axis=-1)
    return jnp.asarray(np.concatenate([upper, lower], axis=1), jnp.bfloat16)


def gather_kernel(band_count, sub_count, kern_count, refs_in, refs_out, scratch, sems):
    raw_screens, values, columns, meta = refs_in
    every_screen, every_line, every_meta = refs_out
    screens, lines, sums = scratch
    far_send, far_recv, mate_send, mate_recv, own_sem = sems
    own, support = screens.shape[0], screens.shape[1]
    width = 2 * support
    line_rows = lines.shape[0]
    band, sub, kern = (lax.axis_index(name) for name in ("band", "sub", "kern"))
    if screens.shape[1] % (16 * sub_count * kern_count):
        fan_count, fan = 1, 0
    else:
        fan_count, fan = sub_count, sub
    part = screens.shape[1] // (fan_count * kern_count)
    mine = pl.ds((fan * kern_count + kern) * part, part)
    peers = [lax.rem(band + d, band_count) for d in range(1, band_count)]
    mates = [
        (lax.rem(sub + s, sub_count), lax.rem(kern + k, kern_count))
        for s in range(fan_count)
        for k in range(kern_count)
        if s or k
    ]
    barrier = pltpu.get_barrier_semaphore()
    for peer in peers:
        pl.semaphore_signal(barrier, inc=1, device_id={"band": peer}, device_id_type=MESH)
    for mate in mates:
        pl.semaphore_signal(
            barrier, inc=1, device_id={"sub": mate[0], "kern": mate[1]}, device_id_type=MESH
        )
    for s in range(own):
        screens[s] = jnp.concatenate([raw_screens[s, 0], raw_screens[s, 1]], axis=-1)
    pl.semaphore_wait(barrier, len(peers) + len(mates))

    here_screen = every_screen.at[pl.ds(band * own, own)]
    here_line = every_line.at[pl.ds(band * line_rows, line_rows)]
    here_meta = every_meta.at[pl.ds(band, 1)]
    own_pairs = [(screens, here_screen), (meta, here_meta), (lines, here_line)]
    far = [[], [], []]
    own_copies = []

    def send(a):
        source, target = own_pairs[a]
        if a == 0:
            source, target = source.at[:, mine], target.at[:, mine]
        for n, peer in enumerate(peers):
            copy = pltpu.make_async_remote_copy(
                src_ref=source,
                dst_ref=target,
                send_sem=far_send.at[n, a],
                recv_sem=far_recv.at[n, a],
                device_id={"band": peer},
                device_id_type=MESH,
            )
            copy.start()
            far[a].append(copy)
        copy = pltpu.make_async_copy(*own_pairs[a], own_sem.at[a])
        copy.start()
        own_copies.append(copy)

    send(0)
    send(1)
    cell = lax.broadcasted_iota(jnp.int32, (width, columns.shape[1]), 0)

    def make_line(b, carry):
        onehot = (cell == columns[pl.ds(b, 1), :]).astype(jnp.float32).astype(jnp.bfloat16)
        line = lax.dot_general(
            values[b], onehot, (((1,), (1,)), ((), ())), preferred_element_type=jnp.float32
        )
        for z in range(2):
            sums[z, pl.ds(b, 1), :] = line[z : z + 1, :]
        return carry

    lax.fori_loop(0, line_rows, make_line, 0, unroll=8)
    lines[...] = (sums[0] + pltpu.roll(sums[1], support, 1)).astype(jnp.bfloat16)
    send(2)
    near = []
    for n in range(len(peers)):
        source_band = lax.rem(band + band_count - 1 - n, band_count)
        piece = every_screen.at[pl.ds(source_band * own, own), mine]
        far[0][n].wait_recv()
        for m, mate in enumerate(mates):
            copy = pltpu.make_async_remote_copy(
                src_ref=piece,
                dst_ref=piece,
                send_sem=mate_send.at[n, m],
                recv_sem=mate_recv.at[n, m],
                device_id={"sub": mate[0], "kern": mate[1]},
                device_id_type=MESH,
            )
            copy.start()
            near.append(copy)
    for n in range(len(peers)):
        far[1][n].wait_recv()
        far[2][n].wait_recv()
    for copy in own_copies:
        copy.wait()
    for copy in near:
        copy.wait()
    for copy in far[0] + far[1] + far[2]:
        copy.wait_send()


def gather(screens, values, columns, meta):
    band_count, sub_count, kern_count = (lax.axis_size(name) for name in ("band", "sub", "kern"))
    own, support, blocks = screens.shape[0], screens.shape[-1], values.shape[0]
    width = 2 * support
    peers, mates = max(band_count - 1, 1), max(sub_count * kern_count - 1, 1)

    def kernel(*refs):
        gather_kernel(
            band_count, sub_count, kern_count, refs[:4], refs[4:7], refs[7:10], refs[10:]
        )

    vmem = pl.BlockSpec(memory_space=pltpu.VMEM)
    dma = pltpu.SemaphoreType.DMA
    return pl.pallas_call(
        kernel,
        out_shape=[
            jax.ShapeDtypeStruct((band_count * own, support, width), jnp.bfloat16),
            jax.ShapeDtypeStruct((band_count * blocks, width), jnp.bfloat16),
            jax.ShapeDtypeStruct((band_count,) + meta.shape[1:], meta.dtype),
        ],
        in_specs=[vmem] * 4,
        out_specs=[vmem] * 3,
        scratch_shapes=[
            pltpu.VMEM((own, support, width), jnp.bfloat16),
            pltpu.VMEM((blocks, width), jnp.bfloat16),
            pltpu.VMEM((2, blocks, width), jnp.float32),
            dma((peers, 3)),
            dma((peers, 3)),
            dma((peers, mates)),
            dma((peers, mates)),
            dma((3,)),
        ],
        compiler_params=pltpu.CompilerParams(
            collective_id=0, has_side_effects=True, vmem_limit_bytes=32 * 1024 * 1024
        ),
    )(screens, values, columns, meta)


def sum_kernel(sub_count, kern_count, grid, out, core_out, core_in, far_out, far_in, sems):
    core_send, core_recv, far_send, far_recv = sems
    rows = out.shape[1]
    step = rows // SUM_PARTS
    sub, kern = lax.axis_index("sub"), lax.axis_index("kern")
    cores = [lax.rem(kern + k, kern_count) for k in range(1, kern_count)]
    subs = [lax.rem(sub + s, sub_count) for s in range(1, sub_count)]
    barrier = pltpu.get_barrier_semaphore()
    for core in cores:
        pl.semaphore_signal(barrier, inc=1, device_id={"kern": core}, device_id_type=MESH)
    for other in subs:
        pl.semaphore_signal(barrier, inc=1, device_id={"sub": other}, device_id_type=MESH)
    pl.semaphore_wait(barrier, len(cores) + len(subs))

    def rows_of(owner_sub, owner_kern, part):
        start = (owner_sub * kern_count + owner_kern) * rows + part * step
        return pl.ds(pl.multiple_of(start, step), step)

    parts = [(z, p) for z in range(2) for p in range(SUM_PARTS)]
    order = [(s, owner) for s, owner in enumerate(subs)] + [(len(subs), sub)]
    near, far = {}, {}
    for s, owner in order:
        for z, p in parts:
            for k, core in enumerate(cores):
                spot = (s, k, z, pl.ds(p * step, step))
                core_out[spot] = grid[z, rows_of(owner, core, p)].astype(jnp.bfloat16)
                copy = pltpu.make_async_remote_copy(
                    src_ref=core_out.at[spot],
                    dst_ref=core_in.at[spot],
                    send_sem=core_send.at[s, k, z, p],
                    recv_sem=core_recv.at[s, k, z, p],
                    device_id={"kern": core},
                    device_id_type=MESH,
                )
                copy.start()
                near[s, k, z, p] = copy

    def chip_total(s, owner, z, p):
        total = grid[z, rows_of(owner, kern, p)]
        for k in range(len(cores)):
            near[s, k, z, p].wait_recv()
            total += core_in[s, k, z, pl.ds(p * step, step)].astype(jnp.float32)
        return total

    for s, owner in order[:-1]:
        for z, p in parts:
            spot = (s, z, pl.ds(p * step, step))
            far_out[spot] = chip_total(s, owner, z, p).astype(jnp.bfloat16)
            copy = pltpu.make_async_remote_copy(
                src_ref=far_out.at[spot],
                dst_ref=far_in.at[spot],
                send_sem=far_send.at[s, z, p],
                recv_sem=far_recv.at[s, z, p],
                device_id={"sub": owner},
                device_id_type=MESH,
            )
            copy.start()
            far[s, z, p] = copy
    for z, p in parts:
        out[z, pl.ds(p * step, step)] = chip_total(len(subs), sub, z, p)
    for z, p in parts:
        for s in range(len(subs)):
            far[s, z, p].wait_recv()
            out[z, pl.ds(p * step, step)] += far_in[s, z, pl.ds(p * step, step)].astype(
                jnp.float32
            )
    for copy in [*near.values(), *far.values()]:
        copy.wait_send()


def sum_rows(grid):
    sub_count, kern_count = lax.axis_size("sub"), lax.axis_size("kern")
    rows = grid.shape[1] // (sub_count * kern_count)
    subs, cores = max(sub_count - 1, 1), max(kern_count - 1, 1)

    def kernel(*refs):
        sum_kernel(sub_count, kern_count, *refs[:6], refs[6:])

    vmem = pl.BlockSpec(memory_space=pltpu.VMEM)
    dma = pltpu.SemaphoreType.DMA
    part = (2, rows, grid.shape[2])
    return pl.pallas_call(
        kernel,
        out_shape=jax.ShapeDtypeStruct(part, jnp.float32),
        in_specs=[vmem],
        out_specs=vmem,
        scratch_shapes=[
            pltpu.VMEM((sub_count, cores) + part, jnp.bfloat16),
            pltpu.VMEM((sub_count, cores) + part, jnp.bfloat16),
            pltpu.VMEM((subs,) + part, jnp.bfloat16),
            pltpu.VMEM((subs,) + part, jnp.bfloat16),
            dma((sub_count, cores, 2, SUM_PARTS)),
            dma((sub_count, cores, 2, SUM_PARTS)),
            dma((subs, 2, SUM_PARTS)),
            dma((subs, 2, SUM_PARTS)),
        ],
        compiler_params=pltpu.CompilerParams(
            collective_id=1, has_side_effects=True, vmem_limit_bytes=32 * 1024 * 1024
        ),
    )(grid)


def grid_kernel(
    support, blocks, meta, screens, lines, rows_tab, cols_tab, grid, hats, line_rows, picked
):
    width = 2 * support
    window = support + SUBLANES
    sources = meta.shape[0]
    me = lax.axis_index("band")
    lane = lax.broadcasted_iota(jnp.int32, (support, width), 1)

    def make_hat(s, carry):
        upper = screens[s].astype(jnp.float32)
        turned = pltpu.roll(upper, support, 1)
        lower = jnp.where(lane < support, -turned, turned)
        hats[s, 0:support, :] = upper.astype(jnp.bfloat16)
        hats[s, support:width, :] = lower.astype(jnp.bfloat16)
        return carry

    lax.fori_loop(0, screens.shape[0], make_hat, 0, unroll=8)
    grid[...] = jnp.zeros_like(grid)
    packed = lines[...].astype(jnp.float32)
    real_half = lax.broadcasted_iota(jnp.int32, packed.shape, 1) < support
    line_rows[0] = jnp.where(real_half, packed, 0.0)
    line_rows[1] = jnp.where(real_half, pltpu.roll(packed, support, 1), 0.0)

    def pick_source(source, count):
        for b in range(blocks):
            picked[count] = source * blocks + b
            count = count + (meta[source, 0, b] == me).astype(jnp.int32)
        return count

    count = lax.fori_loop(0, sources, pick_source, jnp.int32(0))
    for k in range(GROUP):
        picked[count + k] = 0
    lane_window = lax.broadcasted_iota(jnp.int32, (window, width), 1)

    def turn(g, carry):
        places, lefts, halves, kernels, patches = [], [], [], [], []
        for k in range(GROUP):
            slot = g * GROUP + k
            i = picked[slot]
            keep = (slot < count).astype(jnp.float32)
            source, b = lax.div(i, blocks), lax.rem(i, blocks)
            screen, row_off, col_off, row, col = (meta[source, f, b] for f in range(1, 6))
            row_at = jnp.minimum(row // SUBLANES, (BR - window) // SUBLANES)
            col_at = jnp.minimum(col // width, NCOL // width - 2)
            row_shift = row - row_at * SUBLANES
            places.append((row_at, col_at, col - col_at * width))
            lefts.append((i, keep, col_off))
            halves.append(
                jnp.dot(
                    rows_tab[row_off * (SUBLANES + 1) + row_shift],
                    hats[screen],
                    preferred_element_type=jnp.float32,
                ).astype(jnp.bfloat16)
            )
        for (i, keep, col_off), half in zip(lefts, halves):
            kernels.append(
                jnp.dot(half, cols_tab[col_off], preferred_element_type=jnp.float32).astype(
                    jnp.bfloat16
                )
            )
        for (i, keep, col_off), kernel in zip(lefts, kernels):
            spread = [
                pltpu.roll(
                    jnp.broadcast_to(
                        line_rows[z, pl.ds(i, 1), :] * keep, (support, width)
                    ),
                    0,
                    1,
                    stride=1,
                    stride_axis=0,
                )
                for z in range(2)
            ]
            toeplitz = jnp.concatenate(
                [
                    jnp.concatenate([spread[0], spread[1]], axis=1),
                    jnp.concatenate([-spread[1], spread[0]], axis=1),
                ],
                axis=0,
            ).astype(jnp.bfloat16)
            patches.append(jnp.dot(kernel, toeplitz, preferred_element_type=jnp.float32))
        for patch, (row_at, col_at, col_shift) in zip(patches, places):
            rows = pl.ds(pl.multiple_of(row_at * SUBLANES, SUBLANES), window)
            left = pl.ds(pl.multiple_of(col_at * width, width), width)
            right = pl.ds(pl.multiple_of(col_at * width + width, width), width)
            for z in range(2):
                turned = pltpu.roll(
                    patch[:window, z * width : (z + 1) * width], lax.rem(col_shift, width), 1
                )
                inside = lane_window >= col_shift
                grid[z, rows, left] += jnp.where(inside, turned, 0.0)
                grid[z, rows, right] += jnp.where(inside, 0.0, turned)
        return carry

    lax.fori_loop(0, (count + GROUP - 1) // GROUP, turn, 0)


def body(
    screens, visibilities, vis_columns, band_route, screen_choice, offsets, row_cell, col_cell
):
    support = screens.shape[-1]
    width = 2 * support
    tables = dft_tables(support)
    patch_rows = -(-(support + SUBLANES) // 16) * 16
    meta = jnp.stack(
        [band_route[:, 0], screen_choice, offsets[:, 0], offsets[:, 1], row_cell, col_cell]
    )
    blocks = meta.shape[1]
    meta = jnp.pad(meta, ((0, SUBLANES - meta.shape[0]), (0, -blocks % 128)))[None]
    every_screen, every_line, every_meta = gather(screens, visibilities, vis_columns, meta)
    vmem = pl.BlockSpec(memory_space=pltpu.VMEM)
    grid_band = pl.pallas_call(
        functools.partial(grid_kernel, support, blocks),
        out_shape=jax.ShapeDtypeStruct((2, BR, NCOL), jnp.float32),
        in_specs=[pl.BlockSpec(memory_space=pltpu.SMEM), vmem, vmem, vmem, vmem],
        out_specs=vmem,
        scratch_shapes=[
            pltpu.VMEM((every_screen.shape[0], width, width), jnp.bfloat16),
            pltpu.VMEM((2,) + every_line.shape, jnp.float32),
            pltpu.SMEM((every_meta.shape[0] * blocks + GROUP,), jnp.int32),
        ],
        compiler_params=pltpu.CompilerParams(vmem_limit_bytes=32 * 1024 * 1024),
    )(every_meta, every_screen, every_line, row_tables(tables, patch_rows), col_tables(tables))
    return sum_rows(grid_band)


def solution(mesh):
    in_specs = (
        P("band", None, None, None),
        P(("grp", "band", "sub", "kern"), None, None),
        P(("grp", "band", "sub", "kern"), None),
        P(("grp", "band", "sub", "kern"), None),
        P(("grp", "band", "sub", "kern")),
        P(("grp", "band", "sub", "kern"), None),
        P(("grp", "band", "sub", "kern")),
        P(("grp", "band", "sub", "kern")),
    )
    out_specs = P(None, ("grp", "band", "sub", "kern"), None)
    return jax.shard_map(body, mesh=mesh, in_specs=in_specs, out_specs=out_specs, check_vma=False)
```

```python
import functools
import math

import jax
import jax.numpy as jnp
import numpy as np
from jax import lax
from jax.experimental import pallas as pl
from jax.experimental.pallas import tpu as pltpu
from jax.sharding import PartitionSpec as P

OVERS = 8
BR = 256
NCOL = 1024
SUBLANES = 8
GROUP = 8
SUM_PARTS = 2
MESH = pl.DeviceIdType.MESH


def dft_tables(support):
    centred = np.arange(support, dtype=np.float32) - np.float32(support // 2)
    fractions = np.arange(OVERS, dtype=np.float32) / np.float32(OVERS)
    frequency = centred[None, :, None] + fractions[:, None, None]
    phases = np.float32(-2.0 * math.pi) * frequency * centred[None, None, :] / np.float32(support)
    tables = np.stack([np.cos(phases), np.sin(phases)], axis=1) / np.float32(support)
    return tables.astype(jnp.bfloat16).astype(np.float32)


def row_tables(tables, patch_rows):
    support = tables.shape[-1]
    shifted = np.zeros((OVERS, SUBLANES + 1, patch_rows, 2 * support), np.float32)
    wide = np.concatenate([tables[:, 0], tables[:, 1]], axis=-1)
    for shift in range(SUBLANES + 1):
        shifted[:, shift, shift : shift + support] = wide
    return jnp.asarray(shifted.reshape(-1, patch_rows, 2 * support), jnp.bfloat16)


def col_tables(tables):
    real, imag = tables[:, 0].swapaxes(1, 2), tables[:, 1].swapaxes(1, 2)
    upper = np.concatenate([real, imag], axis=-1)
    lower = np.concatenate([-imag, real], axis=-1)
    return jnp.asarray(np.concatenate([upper, lower], axis=1), jnp.bfloat16)


def gather_kernel(band_count, sub_count, kern_count, refs_in, refs_out, scratch, sems):
    every_screen, every_line, every_meta = refs_out
    screens, lines, sums, meta = scratch[:4]
    raw_screens, values, columns, *indices = scratch[4:]
    far_send, far_recv, mate_send, mate_recv, own_sem, load_sem = sems
    loads = [
        pltpu.make_async_copy(source, target, load_sem.at[n])
        for n, (source, target) in enumerate(zip(refs_in, scratch[4:]))
    ]
    for load in loads:
        load.start()
    own, support = screens.shape[0], screens.shape[1]
    width = 2 * support
    line_rows = lines.shape[0]
    band, sub, kern = (lax.axis_index(name) for name in ("band", "sub", "kern"))
    if screens.shape[1] % (16 * sub_count * kern_count):
        fan_count, fan = 1, 0
    else:
        fan_count, fan = sub_count, sub
    part = screens.shape[1] // (fan_count * kern_count)
    mine = pl.ds((fan * kern_count + kern) * part, part)
    peers = [lax.rem(band + d, band_count) for d in range(1, band_count)]
    mates = [
        (lax.rem(sub + s, sub_count), lax.rem(kern + k, kern_count))
        for s in range(fan_count)
        for k in range(kern_count)
        if s or k
    ]
    barrier = pltpu.get_barrier_semaphore()
    for peer in peers:
        pl.semaphore_signal(barrier, inc=1, device_id={"band": peer}, device_id_type=MESH)
    for mate in mates:
        pl.semaphore_signal(
            barrier, inc=1, device_id={"sub": mate[0], "kern": mate[1]}, device_id_type=MESH
        )
    for load in loads:
        load.wait()
    for s in range(own):
        screens[s] = jnp.concatenate([raw_screens[s, 0], raw_screens[s, 1]], axis=-1)
    field = 0
    for index in indices:
        meta[0, field : field + index.shape[0], 0 : index.shape[1]] = index[...]
        field += index.shape[0]
    pl.semaphore_wait(barrier, len(peers) + len(mates))

    here_screen = every_screen.at[pl.ds(band * own, own)]
    here_line = every_line.at[pl.ds(band * line_rows, line_rows)]
    here_meta = every_meta.at[pl.ds(band, 1)]
    own_pairs = [(screens, here_screen), (meta, here_meta), (lines, here_line)]
    far = [[], [], []]
    own_copies = []

    def send(a):
        source, target = own_pairs[a]
        if a == 0:
            source, target = source.at[:, mine], target.at[:, mine]
        for n, peer in enumerate(peers):
            copy = pltpu.make_async_remote_copy(
                src_ref=source,
                dst_ref=target,
                send_sem=far_send.at[n, a],
                recv_sem=far_recv.at[n, a],
                device_id={"band": peer},
                device_id_type=MESH,
            )
            copy.start()
            far[a].append(copy)
        copy = pltpu.make_async_copy(*own_pairs[a], own_sem.at[a])
        copy.start()
        own_copies.append(copy)

    send(0)
    send(1)
    cell = lax.broadcasted_iota(jnp.int32, (width, columns.shape[1]), 0)

    together = math.gcd(line_rows, 16)

    def make_lines(g, carry):
        found = []
        for k in range(together):
            b = g * together + k
            onehot = (cell == columns[pl.ds(b, 1), :]).astype(jnp.float32).astype(jnp.bfloat16)
            found.append(
                lax.dot_general(
                    values[b], onehot, (((1,), (1,)), ((), ())), preferred_element_type=jnp.float32
                )
            )
        for k, line in enumerate(found):
            for z in range(2):
                sums[z, pl.ds(g * together + k, 1), :] = line[z : z + 1, :]
        return carry

    lax.fori_loop(0, line_rows // together, make_lines, 0)
    lines[...] = (sums[0] + pltpu.roll(sums[1], support, 1)).astype(jnp.bfloat16)
    send(2)
    near = []
    for n in range(len(peers)):
        source_band = lax.rem(band + band_count - 1 - n, band_count)
        piece = every_screen.at[pl.ds(source_band * own, own), mine]
        far[0][n].wait_recv()
        for m, mate in enumerate(mates):
            copy = pltpu.make_async_remote_copy(
                src_ref=piece,
                dst_ref=piece,
                send_sem=mate_send.at[n, m],
                recv_sem=mate_recv.at[n, m],
                device_id={"sub": mate[0], "kern": mate[1]},
                device_id_type=MESH,
            )
            copy.start()
            near.append(copy)
    for n in range(len(peers)):
        far[1][n].wait_recv()
        far[2][n].wait_recv()
    for copy in own_copies:
        copy.wait()
    for copy in near:
        copy.wait()
    for copy in far[0] + far[1] + far[2]:
        copy.wait_send()


def gather(screens, values, columns, *indices):
    band_count, sub_count, kern_count = (lax.axis_size(name) for name in ("band", "sub", "kern"))
    operands = (screens, values, columns) + indices
    own, support, blocks = screens.shape[0], screens.shape[-1], values.shape[0]
    width = 2 * support
    meta_shape = (SUBLANES, -(-blocks // 128) * 128)
    peers, mates = max(band_count - 1, 1), max(sub_count * kern_count - 1, 1)

    def kernel(*refs):
        n = len(operands)
        gather_kernel(
            band_count,
            sub_count,
            kern_count,
            refs[:n],
            refs[n : n + 3],
            refs[n + 3 : 2 * n + 7],
            refs[2 * n + 7 :],
        )

    vmem = pl.BlockSpec(memory_space=pltpu.VMEM)
    dma = pltpu.SemaphoreType.DMA
    return pl.pallas_call(
        kernel,
        out_shape=[
            jax.ShapeDtypeStruct((band_count * own, support, width), jnp.bfloat16),
            jax.ShapeDtypeStruct((band_count * blocks, width), jnp.bfloat16),
            jax.ShapeDtypeStruct((band_count,) + meta_shape, jnp.int32),
        ],
        in_specs=[pl.BlockSpec(memory_space=pltpu.HBM)] * len(operands),
        out_specs=[vmem] * 3,
        scratch_shapes=[
            pltpu.VMEM((own, support, width), jnp.bfloat16),
            pltpu.VMEM((blocks, width), jnp.bfloat16),
            pltpu.VMEM((2, blocks, width), jnp.float32),
            pltpu.VMEM((1,) + meta_shape, jnp.int32),
            *[pltpu.VMEM(x.shape, x.dtype) for x in operands],
            dma((peers, 3)),
            dma((peers, 3)),
            dma((peers, mates)),
            dma((peers, mates)),
            dma((3,)),
            dma((len(operands),)),
        ],
        compiler_params=pltpu.CompilerParams(
            collective_id=0, has_side_effects=True, vmem_limit_bytes=60 * 1024 * 1024
        ),
    )(*operands)


def sum_kernel(sub_count, kern_count, grid, out, core_out, core_in, far_out, far_in, sems):
    core_send, core_recv, far_send, far_recv = sems
    rows = out.shape[1]
    step = rows // SUM_PARTS
    sub, kern = lax.axis_index("sub"), lax.axis_index("kern")
    cores = [lax.rem(kern + k, kern_count) for k in range(1, kern_count)]
    subs = [lax.rem(sub + s, sub_count) for s in range(1, sub_count)]
    barrier = pltpu.get_barrier_semaphore()
    for core in cores:
        pl.semaphore_signal(barrier, inc=1, device_id={"kern": core}, device_id_type=MESH)
    for other in subs:
        pl.semaphore_signal(barrier, inc=1, device_id={"sub": other}, device_id_type=MESH)
    pl.semaphore_wait(barrier, len(cores) + len(subs))

    def rows_of(owner_sub, owner_kern, part):
        start = (owner_sub * kern_count + owner_kern) * rows + part * step
        return pl.ds(pl.multiple_of(start, step), step)

    parts = [(z, p) for z in range(2) for p in range(SUM_PARTS)]
    order = [(s, owner) for s, owner in enumerate(subs)] + [(len(subs), sub)]
    near, far = {}, {}
    for s, owner in order:
        for z, p in parts:
            for k, core in enumerate(cores):
                spot = (s, k, z, pl.ds(p * step, step))
                core_out[spot] = grid[z, rows_of(owner, core, p)].astype(jnp.bfloat16)
                copy = pltpu.make_async_remote_copy(
                    src_ref=core_out.at[spot],
                    dst_ref=core_in.at[spot],
                    send_sem=core_send.at[s, k, z, p],
                    recv_sem=core_recv.at[s, k, z, p],
                    device_id={"kern": core},
                    device_id_type=MESH,
                )
                copy.start()
                near[s, k, z, p] = copy

    def chip_total(s, owner, z, p):
        total = grid[z, rows_of(owner, kern, p)]
        for k in range(len(cores)):
            near[s, k, z, p].wait_recv()
            total += core_in[s, k, z, pl.ds(p * step, step)].astype(jnp.float32)
        return total

    for s, owner in order[:-1]:
        for z, p in parts:
            spot = (s, z, pl.ds(p * step, step))
            far_out[spot] = chip_total(s, owner, z, p).astype(jnp.bfloat16)
            copy = pltpu.make_async_remote_copy(
                src_ref=far_out.at[spot],
                dst_ref=far_in.at[spot],
                send_sem=far_send.at[s, z, p],
                recv_sem=far_recv.at[s, z, p],
                device_id={"sub": owner},
                device_id_type=MESH,
            )
            copy.start()
            far[s, z, p] = copy
    for z, p in parts:
        out[z, pl.ds(p * step, step)] = chip_total(len(subs), sub, z, p)
    for z, p in parts:
        for s in range(len(subs)):
            far[s, z, p].wait_recv()
            out[z, pl.ds(p * step, step)] += far_in[s, z, pl.ds(p * step, step)].astype(
                jnp.float32
            )
    for copy in [*near.values(), *far.values()]:
        copy.wait_send()


def sum_rows(grid):
    sub_count, kern_count = lax.axis_size("sub"), lax.axis_size("kern")
    rows = grid.shape[1] // (sub_count * kern_count)
    subs, cores = max(sub_count - 1, 1), max(kern_count - 1, 1)

    def kernel(*refs):
        sum_kernel(sub_count, kern_count, *refs[:6], refs[6:])

    vmem = pl.BlockSpec(memory_space=pltpu.VMEM)
    dma = pltpu.SemaphoreType.DMA
    part = (2, rows, grid.shape[2])
    return pl.pallas_call(
        kernel,
        out_shape=jax.ShapeDtypeStruct(part, jnp.float32),
        in_specs=[vmem],
        out_specs=vmem,
        scratch_shapes=[
            pltpu.VMEM((sub_count, cores) + part, jnp.bfloat16),
            pltpu.VMEM((sub_count, cores) + part, jnp.bfloat16),
            pltpu.VMEM((subs,) + part, jnp.bfloat16),
            pltpu.VMEM((subs,) + part, jnp.bfloat16),
            dma((sub_count, cores, 2, SUM_PARTS)),
            dma((sub_count, cores, 2, SUM_PARTS)),
            dma((subs, 2, SUM_PARTS)),
            dma((subs, 2, SUM_PARTS)),
        ],
        compiler_params=pltpu.CompilerParams(
            collective_id=1, has_side_effects=True, vmem_limit_bytes=60 * 1024 * 1024
        ),
    )(grid)


def grid_kernel(
    support,
    blocks,
    meta,
    screens,
    lines,
    rows_hbm,
    cols_hbm,
    grid,
    rows_tab,
    cols_tab,
    table_sem,
    hats,
    line_rows,
    picked,
):
    tables = [
        pltpu.make_async_copy(rows_hbm, rows_tab, table_sem.at[0]),
        pltpu.make_async_copy(cols_hbm, cols_tab, table_sem.at[1]),
    ]
    for table in tables:
        table.start()
    width = 2 * support
    window = support + SUBLANES
    sources = meta.shape[0]
    me = lax.axis_index("band")
    lane = lax.broadcasted_iota(jnp.int32, (support, width), 1)

    def make_hat(s, carry):
        upper = screens[s].astype(jnp.float32)
        turned = pltpu.roll(upper, support, 1)
        lower = jnp.where(lane < support, -turned, turned)
        hats[s, 0:support, :] = upper.astype(jnp.bfloat16)
        hats[s, support:width, :] = lower.astype(jnp.bfloat16)
        return carry

    lax.fori_loop(0, screens.shape[0], make_hat, 0, unroll=8)
    grid[...] = jnp.zeros_like(grid)
    packed = lines[...].astype(jnp.float32)
    real_half = lax.broadcasted_iota(jnp.int32, packed.shape, 1) < support
    line_rows[0] = jnp.where(real_half, packed, 0.0)
    line_rows[1] = jnp.where(real_half, pltpu.roll(packed, support, 1), 0.0)

    def pick_source(source, count):
        for b in range(blocks):
            picked[count] = source * blocks + b
            count = count + (meta[source, 0, b] == me).astype(jnp.int32)
        return count

    count = lax.fori_loop(0, sources, pick_source, jnp.int32(0))
    for k in range(GROUP):
        picked[count + k] = 0
    lane_window = lax.broadcasted_iota(jnp.int32, (window, width), 1)

    for table in tables:
        table.wait()

    def turn(g, carry):
        places, lefts, halves, kernels, patches = [], [], [], [], []
        for k in range(GROUP):
            slot = g * GROUP + k
            i = picked[slot]
            keep = (slot < count).astype(jnp.float32)
            source, b = lax.div(i, blocks), lax.rem(i, blocks)
            screen, row_off, col_off, row, col = (meta[source, f, b] for f in range(1, 6))
            row_at = jnp.minimum(row // SUBLANES, (BR - window) // SUBLANES)
            col_at = jnp.minimum(col // width, NCOL // width - 2)
            row_shift = row - row_at * SUBLANES
            places.append((row_at, col_at, col - col_at * width))
            lefts.append((i, keep, col_off))
            halves.append(
                jnp.dot(
                    rows_tab[row_off * (SUBLANES + 1) + row_shift],
                    hats[screen],
                    preferred_element_type=jnp.float32,
                ).astype(jnp.bfloat16)
            )
        for (i, keep, col_off), half in zip(lefts, halves):
            kernels.append(
                jnp.dot(half, cols_tab[col_off], preferred_element_type=jnp.float32).astype(
                    jnp.bfloat16
                )
            )
        for (i, keep, col_off), kernel in zip(lefts, kernels):
            spread = [
                pltpu.roll(
                    jnp.broadcast_to(
                        line_rows[z, pl.ds(i, 1), :] * keep, (support, width)
                    ),
                    0,
                    1,
                    stride=1,
                    stride_axis=0,
                )
                for z in range(2)
            ]
            toeplitz = jnp.concatenate(
                [
                    jnp.concatenate([spread[0], spread[1]], axis=1),
                    jnp.concatenate([-spread[1], spread[0]], axis=1),
                ],
                axis=0,
            ).astype(jnp.bfloat16)
            patches.append(jnp.dot(kernel, toeplitz, preferred_element_type=jnp.float32))
        for patch, (row_at, col_at, col_shift) in zip(patches, places):
            rows = pl.ds(pl.multiple_of(row_at * SUBLANES, SUBLANES), window)
            left = pl.ds(pl.multiple_of(col_at * width, width), width)
            right = pl.ds(pl.multiple_of(col_at * width + width, width), width)
            for z in range(2):
                turned = pltpu.roll(
                    patch[:window, z * width : (z + 1) * width], lax.rem(col_shift, width), 1
                )
                inside = lane_window >= col_shift
                grid[z, rows, left] += jnp.where(inside, turned, 0.0)
                grid[z, rows, right] += jnp.where(inside, 0.0, turned)
        return carry

    lax.fori_loop(0, (count + GROUP - 1) // GROUP, turn, 0)


def body(
    screens, visibilities, vis_columns, band_route, screen_choice, offsets, row_cell, col_cell
):
    support = screens.shape[-1]
    width = 2 * support
    tables = dft_tables(support)
    patch_rows = -(-(support + SUBLANES) // 16) * 16
    blocks = visibilities.shape[0]
    every_screen, every_line, every_meta = gather(
        screens,
        visibilities,
        vis_columns,
        band_route.T,
        screen_choice[None],
        offsets.T,
        row_cell[None],
        col_cell[None],
    )
    row_table, col_table = row_tables(tables, patch_rows), col_tables(tables)
    hbm = pl.BlockSpec(memory_space=pltpu.HBM)
    vmem = pl.BlockSpec(memory_space=pltpu.VMEM)
    grid_band = pl.pallas_call(
        functools.partial(grid_kernel, support, blocks),
        out_shape=jax.ShapeDtypeStruct((2, BR, NCOL), jnp.float32),
        in_specs=[pl.BlockSpec(memory_space=pltpu.SMEM), vmem, vmem, hbm, hbm],
        out_specs=vmem,
        scratch_shapes=[
            pltpu.VMEM(row_table.shape, jnp.bfloat16),
            pltpu.VMEM(col_table.shape, jnp.bfloat16),
            pltpu.SemaphoreType.DMA((2,)),
            pltpu.VMEM((every_screen.shape[0], width, width), jnp.bfloat16),
            pltpu.VMEM((2,) + every_line.shape, jnp.float32),
            pltpu.SMEM((every_meta.shape[0] * blocks + GROUP,), jnp.int32),
        ],
        compiler_params=pltpu.CompilerParams(vmem_limit_bytes=60 * 1024 * 1024),
    )(every_meta, every_screen, every_line, row_table, col_table)
    return sum_rows(grid_band)


def solution(mesh):
    in_specs = (
        P("band", None, None, None),
        P(("grp", "band", "sub", "kern"), None, None),
        P(("grp", "band", "sub", "kern"), None),
        P(("grp", "band", "sub", "kern"), None),
        P(("grp", "band", "sub", "kern")),
        P(("grp", "band", "sub", "kern"), None),
        P(("grp", "band", "sub", "kern")),
        P(("grp", "band", "sub", "kern")),
    )
    out_specs = P(None, ("grp", "band", "sub", "kern"), None)
    return jax.shard_map(body, mesh=mesh, in_specs=in_specs, out_specs=out_specs, check_vma=False)
```

```python
import functools
import math

import jax
import jax.numpy as jnp
import numpy as np
from jax import lax
from jax.experimental import pallas as pl
from jax.experimental.pallas import tpu as pltpu
from jax.sharding import PartitionSpec as P

OVERS = 8
BR = 256
NCOL = 1024
SUBLANES = 8
GROUP = 8
SUM_PARTS = 2
MESH = pl.DeviceIdType.MESH


def dft_tables(support):
    centred = np.arange(support, dtype=np.float32) - np.float32(support // 2)
    fractions = np.arange(OVERS, dtype=np.float32) / np.float32(OVERS)
    frequency = centred[None, :, None] + fractions[:, None, None]
    phases = np.float32(-2.0 * math.pi) * frequency * centred[None, None, :] / np.float32(support)
    tables = np.stack([np.cos(phases), np.sin(phases)], axis=1) / np.float32(support)
    return tables.astype(jnp.bfloat16).astype(np.float32)


def row_tables(tables, patch_rows):
    support = tables.shape[-1]
    shifted = np.zeros((OVERS, SUBLANES + 1, patch_rows, 2 * support), np.float32)
    wide = np.concatenate([tables[:, 0], tables[:, 1]], axis=-1)
    for shift in range(SUBLANES + 1):
        shifted[:, shift, shift : shift + support] = wide
    return jnp.asarray(shifted.reshape(-1, patch_rows, 2 * support), jnp.bfloat16)


def col_tables(tables):
    real, imag = tables[:, 0].swapaxes(1, 2), tables[:, 1].swapaxes(1, 2)
    upper = np.concatenate([real, imag], axis=-1)
    lower = np.concatenate([-imag, real], axis=-1)
    return jnp.asarray(np.concatenate([upper, lower], axis=1), jnp.bfloat16)


def gather_kernel(band_count, sub_count, kern_count, refs_in, refs_out, scratch, sems):
    every_screen, every_line, every_meta = refs_out
    screens, lines, sums, meta = scratch[:4]
    raw_screens, values, columns, *indices = scratch[4:]
    far_send, far_recv, mate_send, mate_recv, own_sem, load_sem = sems
    loads = [
        pltpu.make_async_copy(source, target, load_sem.at[n])
        for n, (source, target) in enumerate(zip(refs_in, scratch[4:]))
    ]
    for load in loads:
        load.start()
    own, support = screens.shape[0], screens.shape[1]
    width = 2 * support
    line_rows = lines.shape[0]
    band, sub, kern = (lax.axis_index(name) for name in ("band", "sub", "kern"))
    if screens.shape[1] % (16 * sub_count * kern_count):
        fan_count, fan = 1, 0
    else:
        fan_count, fan = sub_count, sub
    part = screens.shape[1] // (fan_count * kern_count)
    mine = pl.ds((fan * kern_count + kern) * part, part)
    peers = [lax.rem(band + d, band_count) for d in range(1, band_count)]
    mates = [
        (lax.rem(sub + s, sub_count), lax.rem(kern + k, kern_count))
        for s in range(fan_count)
        for k in range(kern_count)
        if s or k
    ]
    barrier = pltpu.get_barrier_semaphore()
    for peer in peers:
        pl.semaphore_signal(barrier, inc=1, device_id={"band": peer}, device_id_type=MESH)
    for mate in mates:
        pl.semaphore_signal(
            barrier, inc=1, device_id={"sub": mate[0], "kern": mate[1]}, device_id_type=MESH
        )
    for load in loads:
        load.wait()
    for s in range(own):
        screens[s] = jnp.concatenate([raw_screens[s, 0], raw_screens[s, 1]], axis=-1)
    field = 0
    for index in indices:
        meta[0, field : field + index.shape[0], 0 : index.shape[1]] = index[...]
        field += index.shape[0]
    pl.semaphore_wait(barrier, len(peers) + len(mates))

    here_screen = every_screen.at[pl.ds(band * own, own)]
    here_line = every_line.at[pl.ds(band * line_rows, line_rows)]
    here_meta = every_meta.at[pl.ds(band, 1)]
    own_pairs = [(screens, here_screen), (meta, here_meta), (lines, here_line)]
    far = [[], [], []]
    own_copies = []

    def send(a):
        source, target = own_pairs[a]
        if a == 0:
            source, target = source.at[:, mine], target.at[:, mine]
        for n, peer in enumerate(peers):
            copy = pltpu.make_async_remote_copy(
                src_ref=source,
                dst_ref=target,
                send_sem=far_send.at[n, a],
                recv_sem=far_recv.at[n, a],
                device_id={"band": peer},
                device_id_type=MESH,
            )
            copy.start()
            far[a].append(copy)
        copy = pltpu.make_async_copy(*own_pairs[a], own_sem.at[a])
        copy.start()
        own_copies.append(copy)

    send(0)
    send(1)
    cell = lax.broadcasted_iota(jnp.int32, (width, columns.shape[1]), 0)

    together = math.gcd(line_rows, 16)

    def make_lines(g, carry):
        found = []
        for k in range(together):
            b = g * together + k
            onehot = (cell == columns[pl.ds(b, 1), :]).astype(jnp.float32).astype(jnp.bfloat16)
            found.append(
                lax.dot_general(
                    values[b], onehot, (((1,), (1,)), ((), ())), preferred_element_type=jnp.float32
                )
            )
        for k, line in enumerate(found):
            for z in range(2):
                sums[z, pl.ds(g * together + k, 1), :] = line[z : z + 1, :]
        return carry

    lax.fori_loop(0, line_rows // together, make_lines, 0)
    lines[...] = (sums[0] + pltpu.roll(sums[1], support, 1)).astype(jnp.bfloat16)
    send(2)
    near = []
    for n in range(len(peers)):
        source_band = lax.rem(band + band_count - 1 - n, band_count)
        piece = every_screen.at[pl.ds(source_band * own, own), mine]
        far[0][n].wait_recv()
        for m, mate in enumerate(mates):
            copy = pltpu.make_async_remote_copy(
                src_ref=piece,
                dst_ref=piece,
                send_sem=mate_send.at[n, m],
                recv_sem=mate_recv.at[n, m],
                device_id={"sub": mate[0], "kern": mate[1]},
                device_id_type=MESH,
            )
            copy.start()
            near.append(copy)
    for n in range(len(peers)):
        far[1][n].wait_recv()
        far[2][n].wait_recv()
    for copy in own_copies:
        copy.wait()
    for copy in near:
        copy.wait()
    for copy in far[0] + far[1] + far[2]:
        copy.wait_send()


def gather(screens, values, columns, *indices):
    band_count, sub_count, kern_count = (lax.axis_size(name) for name in ("band", "sub", "kern"))
    operands = (screens, values, columns) + indices
    own, support, blocks = screens.shape[0], screens.shape[-1], values.shape[0]
    width = 2 * support
    meta_shape = (SUBLANES, -(-blocks // 128) * 128)
    peers, mates = max(band_count - 1, 1), max(sub_count * kern_count - 1, 1)

    def kernel(*refs):
        n = len(operands)
        gather_kernel(
            band_count,
            sub_count,
            kern_count,
            refs[:n],
            refs[n : n + 3],
            refs[n + 3 : 2 * n + 7],
            refs[2 * n + 7 :],
        )

    vmem = pl.BlockSpec(memory_space=pltpu.VMEM)
    dma = pltpu.SemaphoreType.DMA
    return pl.pallas_call(
        kernel,
        out_shape=[
            jax.ShapeDtypeStruct((band_count * own, support, width), jnp.bfloat16),
            jax.ShapeDtypeStruct((band_count * blocks, width), jnp.bfloat16),
            jax.ShapeDtypeStruct((band_count,) + meta_shape, jnp.int32),
        ],
        in_specs=[pl.BlockSpec(memory_space=pltpu.HBM)] * len(operands),
        out_specs=[vmem] * 3,
        scratch_shapes=[
            pltpu.VMEM((own, support, width), jnp.bfloat16),
            pltpu.VMEM((blocks, width), jnp.bfloat16),
            pltpu.VMEM((2, blocks, width), jnp.float32),
            pltpu.VMEM((1,) + meta_shape, jnp.int32),
            *[pltpu.VMEM(x.shape, x.dtype) for x in operands],
            dma((peers, 3)),
            dma((peers, 3)),
            dma((peers, mates)),
            dma((peers, mates)),
            dma((3,)),
            dma((len(operands),)),
        ],
        compiler_params=pltpu.CompilerParams(
            collective_id=0, has_side_effects=True, vmem_limit_bytes=60 * 1024 * 1024
        ),
    )(*operands)


def sum_kernel(
    sub_count, kern_count, grid_hbm, out, core_out, core_in, far_out, far_in, grid, sems
):
    core_send, core_recv, far_send, far_recv, load_sem = sems
    rows = out.shape[1]
    step = rows // SUM_PARTS
    sub, kern = lax.axis_index("sub"), lax.axis_index("kern")
    cores = [lax.rem(kern + k, kern_count) for k in range(1, kern_count)]
    subs = [lax.rem(sub + s, sub_count) for s in range(1, sub_count)]
    loads = {}
    for s, owner in enumerate(subs + [sub]):
        for k, core in enumerate(cores + [kern]):
            span = pl.ds(pl.multiple_of((owner * kern_count + core) * rows, rows), rows)
            loads[s, k] = pltpu.make_async_copy(
                grid_hbm.at[:, span], grid.at[:, span], load_sem.at[s, k]
            )
            loads[s, k].start()
    barrier = pltpu.get_barrier_semaphore()
    for core in cores:
        pl.semaphore_signal(barrier, inc=1, device_id={"kern": core}, device_id_type=MESH)
    for other in subs:
        pl.semaphore_signal(barrier, inc=1, device_id={"sub": other}, device_id_type=MESH)
    pl.semaphore_wait(barrier, len(cores) + len(subs))

    def rows_of(owner_sub, owner_kern, part):
        start = (owner_sub * kern_count + owner_kern) * rows + part * step
        return pl.ds(pl.multiple_of(start, step), step)

    parts = [(z, p) for z in range(2) for p in range(SUM_PARTS)]
    order = [(s, owner) for s, owner in enumerate(subs)] + [(len(subs), sub)]
    near, far = {}, {}
    for s, owner in order:
        for k in range(len(cores)):
            loads[s, k].wait()
        for z, p in parts:
            for k, core in enumerate(cores):
                spot = (s, k, z, pl.ds(p * step, step))
                core_out[spot] = grid[z, rows_of(owner, core, p)].astype(jnp.bfloat16)
                copy = pltpu.make_async_remote_copy(
                    src_ref=core_out.at[spot],
                    dst_ref=core_in.at[spot],
                    send_sem=core_send.at[s, k, z, p],
                    recv_sem=core_recv.at[s, k, z, p],
                    device_id={"kern": core},
                    device_id_type=MESH,
                )
                copy.start()
                near[s, k, z, p] = copy

    def chip_total(s, owner, z, p):
        total = grid[z, rows_of(owner, kern, p)]
        for k in range(len(cores)):
            near[s, k, z, p].wait_recv()
            total += core_in[s, k, z, pl.ds(p * step, step)].astype(jnp.float32)
        return total

    for s in range(len(order)):
        loads[s, len(cores)].wait()
    for s, owner in order[:-1]:
        for z, p in parts:
            spot = (s, z, pl.ds(p * step, step))
            far_out[spot] = chip_total(s, owner, z, p).astype(jnp.bfloat16)
            copy = pltpu.make_async_remote_copy(
                src_ref=far_out.at[spot],
                dst_ref=far_in.at[spot],
                send_sem=far_send.at[s, z, p],
                recv_sem=far_recv.at[s, z, p],
                device_id={"sub": owner},
                device_id_type=MESH,
            )
            copy.start()
            far[s, z, p] = copy
    for z, p in parts:
        out[z, pl.ds(p * step, step)] = chip_total(len(subs), sub, z, p)
    for z, p in parts:
        for s in range(len(subs)):
            far[s, z, p].wait_recv()
            out[z, pl.ds(p * step, step)] += far_in[s, z, pl.ds(p * step, step)].astype(
                jnp.float32
            )
    for copy in [*near.values(), *far.values()]:
        copy.wait_send()


def sum_rows(grid):
    sub_count, kern_count = lax.axis_size("sub"), lax.axis_size("kern")
    rows = grid.shape[1] // (sub_count * kern_count)
    subs, cores = max(sub_count - 1, 1), max(kern_count - 1, 1)

    def kernel(*refs):
        sum_kernel(sub_count, kern_count, *refs[:7], refs[7:])

    vmem = pl.BlockSpec(memory_space=pltpu.VMEM)
    dma = pltpu.SemaphoreType.DMA
    part = (2, rows, grid.shape[2])
    return pl.pallas_call(
        kernel,
        out_shape=jax.ShapeDtypeStruct(part, jnp.float32),
        in_specs=[pl.BlockSpec(memory_space=pltpu.HBM)],
        out_specs=vmem,
        scratch_shapes=[
            pltpu.VMEM((sub_count, cores) + part, jnp.bfloat16),
            pltpu.VMEM((sub_count, cores) + part, jnp.bfloat16),
            pltpu.VMEM((subs,) + part, jnp.bfloat16),
            pltpu.VMEM((subs,) + part, jnp.bfloat16),
            pltpu.VMEM(grid.shape, jnp.float32),
            dma((sub_count, cores, 2, SUM_PARTS)),
            dma((sub_count, cores, 2, SUM_PARTS)),
            dma((subs, 2, SUM_PARTS)),
            dma((subs, 2, SUM_PARTS)),
            dma((sub_count, kern_count)),
        ],
        compiler_params=pltpu.CompilerParams(
            collective_id=1, has_side_effects=True, vmem_limit_bytes=52 * 1024 * 1024
        ),
    )(grid)


def grid_kernel(
    support,
    blocks,
    meta,
    screens,
    lines,
    rows_hbm,
    cols_hbm,
    grid,
    rows_tab,
    cols_tab,
    table_sem,
    hats,
    line_rows,
    picked,
):
    tables = [
        pltpu.make_async_copy(rows_hbm, rows_tab, table_sem.at[0]),
        pltpu.make_async_copy(cols_hbm, cols_tab, table_sem.at[1]),
    ]
    for table in tables:
        table.start()
    width = 2 * support
    window = support + SUBLANES
    sources = meta.shape[0]
    me = lax.axis_index("band")
    lane = lax.broadcasted_iota(jnp.int32, (support, width), 1)

    def make_hat(s, carry):
        upper = screens[s].astype(jnp.float32)
        turned = pltpu.roll(upper, support, 1)
        lower = jnp.where(lane < support, -turned, turned)
        hats[s, 0:support, :] = upper.astype(jnp.bfloat16)
        hats[s, support:width, :] = lower.astype(jnp.bfloat16)
        return carry

    lax.fori_loop(0, screens.shape[0], make_hat, 0, unroll=8)
    grid[...] = jnp.zeros_like(grid)
    packed = lines[...].astype(jnp.float32)
    real_half = lax.broadcasted_iota(jnp.int32, packed.shape, 1) < support
    line_rows[0] = jnp.where(real_half, packed, 0.0)
    line_rows[1] = jnp.where(real_half, pltpu.roll(packed, support, 1), 0.0)

    def pick_source(source, count):
        for b in range(blocks):
            picked[count] = source * blocks + b
            count = count + (meta[source, 0, b] == me).astype(jnp.int32)
        return count

    count = lax.fori_loop(0, sources, pick_source, jnp.int32(0))
    for k in range(GROUP):
        picked[count + k] = 0
    lane_window = lax.broadcasted_iota(jnp.int32, (window, width), 1)

    for table in tables:
        table.wait()

    def turn(g, carry):
        places, lefts, halves, kernels, patches = [], [], [], [], []
        for k in range(GROUP):
            slot = g * GROUP + k
            i = picked[slot]
            keep = (slot < count).astype(jnp.float32)
            source, b = lax.div(i, blocks), lax.rem(i, blocks)
            screen, row_off, col_off, row, col = (meta[source, f, b] for f in range(1, 6))
            row_at = jnp.minimum(row // SUBLANES, (BR - window) // SUBLANES)
            col_at = jnp.minimum(col // width, NCOL // width - 2)
            row_shift = row - row_at * SUBLANES
            places.append((row_at, col_at, col - col_at * width))
            lefts.append((i, keep, col_off))
            halves.append(
                jnp.dot(
                    rows_tab[row_off * (SUBLANES + 1) + row_shift],
                    hats[screen],
                    preferred_element_type=jnp.float32,
                ).astype(jnp.bfloat16)
            )
        for (i, keep, col_off), half in zip(lefts, halves):
            kernels.append(
                jnp.dot(half, cols_tab[col_off], preferred_element_type=jnp.float32).astype(
                    jnp.bfloat16
                )
            )
        for (i, keep, col_off), kernel in zip(lefts, kernels):
            spread = [
                pltpu.roll(
                    jnp.broadcast_to(
                        line_rows[z, pl.ds(i, 1), :] * keep, (support, width)
                    ),
                    0,
                    1,
                    stride=1,
                    stride_axis=0,
                )
                for z in range(2)
            ]
            toeplitz = jnp.concatenate(
                [
                    jnp.concatenate([spread[0], spread[1]], axis=1),
                    jnp.concatenate([-spread[1], spread[0]], axis=1),
                ],
                axis=0,
            ).astype(jnp.bfloat16)
            patches.append(jnp.dot(kernel, toeplitz, preferred_element_type=jnp.float32))
        for patch, (row_at, col_at, col_shift) in zip(patches, places):
            rows = pl.ds(pl.multiple_of(row_at * SUBLANES, SUBLANES), window)
            left = pl.ds(pl.multiple_of(col_at * width, width), width)
            right = pl.ds(pl.multiple_of(col_at * width + width, width), width)
            for z in range(2):
                turned = pltpu.roll(
                    patch[:window, z * width : (z + 1) * width], lax.rem(col_shift, width), 1
                )
                inside = lane_window >= col_shift
                grid[z, rows, left] += jnp.where(inside, turned, 0.0)
                grid[z, rows, right] += jnp.where(inside, 0.0, turned)
        return carry

    lax.fori_loop(0, (count + GROUP - 1) // GROUP, turn, 0)


def body(
    screens, visibilities, vis_columns, band_route, screen_choice, offsets, row_cell, col_cell
):
    support = screens.shape[-1]
    width = 2 * support
    tables = dft_tables(support)
    patch_rows = -(-(support + SUBLANES) // 16) * 16
    blocks = visibilities.shape[0]
    every_screen, every_line, every_meta = gather(
        screens,
        visibilities,
        vis_columns,
        band_route.T,
        screen_choice[None],
        offsets.T,
        row_cell[None],
        col_cell[None],
    )
    row_table, col_table = row_tables(tables, patch_rows), col_tables(tables)
    hbm = pl.BlockSpec(memory_space=pltpu.HBM)
    vmem = pl.BlockSpec(memory_space=pltpu.VMEM)
    grid_band = pl.pallas_call(
        functools.partial(grid_kernel, support, blocks),
        out_shape=jax.ShapeDtypeStruct((2, BR, NCOL), jnp.float32),
        in_specs=[pl.BlockSpec(memory_space=pltpu.SMEM), vmem, vmem, hbm, hbm],
        out_specs=vmem,
        scratch_shapes=[
            pltpu.VMEM(row_table.shape, jnp.bfloat16),
            pltpu.VMEM(col_table.shape, jnp.bfloat16),
            pltpu.SemaphoreType.DMA((2,)),
            pltpu.VMEM((every_screen.shape[0], width, width), jnp.bfloat16),
            pltpu.VMEM((2,) + every_line.shape, jnp.float32),
            pltpu.SMEM((every_meta.shape[0] * blocks + GROUP,), jnp.int32),
        ],
        compiler_params=pltpu.CompilerParams(vmem_limit_bytes=60 * 1024 * 1024),
    )(every_meta, every_screen, every_line, row_table, col_table)
    return sum_rows(grid_band)


def solution(mesh):
    in_specs = (
        P("band", None, None, None),
        P(("grp", "band", "sub", "kern"), None, None),
        P(("grp", "band", "sub", "kern"), None),
        P(("grp", "band", "sub", "kern"), None),
        P(("grp", "band", "sub", "kern")),
        P(("grp", "band", "sub", "kern"), None),
        P(("grp", "band", "sub", "kern")),
        P(("grp", "band", "sub", "kern")),
    )
    out_specs = P(None, ("grp", "band", "sub", "kern"), None)
    return jax.shard_map(body, mesh=mesh, in_specs=in_specs, out_specs=out_specs, check_vma=False)
```

```python
import functools
import math

import jax
import jax.numpy as jnp
import numpy as np
from jax import lax
from jax.experimental import pallas as pl
from jax.experimental.pallas import tpu as pltpu
from jax.sharding import PartitionSpec as P

OVERS = 8
BR = 256
NCOL = 1024
SUBLANES = 8
GROUP = 16
SUM_PARTS = 2
MESH = pl.DeviceIdType.MESH


def dft_tables(support):
    centred = np.arange(support, dtype=np.float32) - np.float32(support // 2)
    fractions = np.arange(OVERS, dtype=np.float32) / np.float32(OVERS)
    frequency = centred[None, :, None] + fractions[:, None, None]
    phases = np.float32(-2.0 * math.pi) * frequency * centred[None, None, :] / np.float32(support)
    tables = np.stack([np.cos(phases), np.sin(phases)], axis=1) / np.float32(support)
    return tables.astype(jnp.bfloat16).astype(np.float32)


def row_tables(tables, patch_rows):
    support = tables.shape[-1]
    shifted = np.zeros((OVERS, SUBLANES + 1, patch_rows, 2 * support), np.float32)
    wide = np.concatenate([tables[:, 0], tables[:, 1]], axis=-1)
    for shift in range(SUBLANES + 1):
        shifted[:, shift, shift : shift + support] = wide
    return jnp.asarray(shifted.reshape(-1, patch_rows, 2 * support), jnp.bfloat16)


def col_tables(tables):
    real, imag = tables[:, 0].swapaxes(1, 2), tables[:, 1].swapaxes(1, 2)
    upper = np.concatenate([real, imag], axis=-1)
    lower = np.concatenate([-imag, real], axis=-1)
    return jnp.asarray(np.concatenate([upper, lower], axis=1), jnp.bfloat16)


def gather_kernel(band_count, sub_count, kern_count, refs_in, refs_out, scratch, sems):
    every_screen, every_line, every_meta = refs_out
    screens, lines, sums, meta = scratch[:4]
    raw_screens, values, columns, *indices = scratch[4:]
    far_send, far_recv, mate_send, mate_recv, own_sem, load_sem = sems
    loads = [
        pltpu.make_async_copy(source, target, load_sem.at[n])
        for n, (source, target) in enumerate(zip(refs_in, scratch[4:]))
    ]
    for load in loads:
        load.start()
    own, support = screens.shape[0], screens.shape[1]
    width = 2 * support
    line_rows = lines.shape[0]
    band, sub, kern = (lax.axis_index(name) for name in ("band", "sub", "kern"))
    if screens.shape[1] % (16 * sub_count * kern_count):
        fan_count, fan = 1, 0
    else:
        fan_count, fan = sub_count, sub
    part = screens.shape[1] // (fan_count * kern_count)
    mine = pl.ds((fan * kern_count + kern) * part, part)
    peers = [lax.rem(band + d, band_count) for d in range(1, band_count)]
    mates = [
        (lax.rem(sub + s, sub_count), lax.rem(kern + k, kern_count))
        for s in range(fan_count)
        for k in range(kern_count)
        if s or k
    ]
    barrier = pltpu.get_barrier_semaphore()
    for peer in peers:
        pl.semaphore_signal(barrier, inc=1, device_id={"band": peer}, device_id_type=MESH)
    for mate in mates:
        pl.semaphore_signal(
            barrier, inc=1, device_id={"sub": mate[0], "kern": mate[1]}, device_id_type=MESH
        )
    for load in loads:
        load.wait()
    for s in range(own):
        screens[s] = jnp.concatenate([raw_screens[s, 0], raw_screens[s, 1]], axis=-1)
    field = 0
    for index in indices:
        meta[0, field : field + index.shape[0], 0 : index.shape[1]] = index[...]
        field += index.shape[0]
    pl.semaphore_wait(barrier, len(peers) + len(mates))

    here_screen = every_screen.at[pl.ds(band * own, own)]
    here_line = every_line.at[pl.ds(band * line_rows, line_rows)]
    here_meta = every_meta.at[pl.ds(band, 1)]
    own_pairs = [(screens, here_screen), (meta, here_meta), (lines, here_line)]
    far = [[], [], []]
    own_copies = []

    def send(a):
        source, target = own_pairs[a]
        if a == 0:
            source, target = source.at[:, mine], target.at[:, mine]
        for n, peer in enumerate(peers):
            copy = pltpu.make_async_remote_copy(
                src_ref=source,
                dst_ref=target,
                send_sem=far_send.at[n, a],
                recv_sem=far_recv.at[n, a],
                device_id={"band": peer},
                device_id_type=MESH,
            )
            copy.start()
            far[a].append(copy)
        copy = pltpu.make_async_copy(*own_pairs[a], own_sem.at[a])
        copy.start()
        own_copies.append(copy)

    send(0)
    send(1)
    cell = lax.broadcasted_iota(jnp.int32, (width, columns.shape[1]), 0)

    together = math.gcd(line_rows, 16)

    def make_lines(g, carry):
        found = []
        for k in range(together):
            b = g * together + k
            onehot = (cell == columns[pl.ds(b, 1), :]).astype(jnp.float32).astype(jnp.bfloat16)
            found.append(
                lax.dot_general(
                    values[b], onehot, (((1,), (1,)), ((), ())), preferred_element_type=jnp.float32
                )
            )
        for k, line in enumerate(found):
            for z in range(2):
                sums[z, pl.ds(g * together + k, 1), :] = line[z : z + 1, :]
        return carry

    lax.fori_loop(0, line_rows // together, make_lines, 0)
    lines[...] = (sums[0] + pltpu.roll(sums[1], support, 1)).astype(jnp.bfloat16)
    send(2)
    near = []
    for n in range(len(peers)):
        source_band = lax.rem(band + band_count - 1 - n, band_count)
        piece = every_screen.at[pl.ds(source_band * own, own), mine]
        far[0][n].wait_recv()
        for m, mate in enumerate(mates):
            copy = pltpu.make_async_remote_copy(
                src_ref=piece,
                dst_ref=piece,
                send_sem=mate_send.at[n, m],
                recv_sem=mate_recv.at[n, m],
                device_id={"sub": mate[0], "kern": mate[1]},
                device_id_type=MESH,
            )
            copy.start()
            near.append(copy)
    for n in range(len(peers)):
        far[1][n].wait_recv()
        far[2][n].wait_recv()
    for copy in own_copies:
        copy.wait()
    for copy in near:
        copy.wait()
    for copy in far[0] + far[1] + far[2]:
        copy.wait_send()


def gather(screens, values, columns, *indices):
    band_count, sub_count, kern_count = (lax.axis_size(name) for name in ("band", "sub", "kern"))
    operands = (screens, values, columns) + indices
    own, support, blocks = screens.shape[0], screens.shape[-1], values.shape[0]
    width = 2 * support
    meta_shape = (SUBLANES, -(-blocks // 128) * 128)
    peers, mates = max(band_count - 1, 1), max(sub_count * kern_count - 1, 1)

    def kernel(*refs):
        n = len(operands)
        gather_kernel(
            band_count,
            sub_count,
            kern_count,
            refs[:n],
            refs[n : n + 3],
            refs[n + 3 : 2 * n + 7],
            refs[2 * n + 7 :],
        )

    vmem = pl.BlockSpec(memory_space=pltpu.VMEM)
    dma = pltpu.SemaphoreType.DMA
    return pl.pallas_call(
        kernel,
        out_shape=[
            jax.ShapeDtypeStruct((band_count * own, support, width), jnp.bfloat16),
            jax.ShapeDtypeStruct((band_count * blocks, width), jnp.bfloat16),
            jax.ShapeDtypeStruct((band_count,) + meta_shape, jnp.int32),
        ],
        in_specs=[pl.BlockSpec(memory_space=pltpu.HBM)] * len(operands),
        out_specs=[vmem] * 3,
        scratch_shapes=[
            pltpu.VMEM((own, support, width), jnp.bfloat16),
            pltpu.VMEM((blocks, width), jnp.bfloat16),
            pltpu.VMEM((2, blocks, width), jnp.float32),
            pltpu.VMEM((1,) + meta_shape, jnp.int32),
            *[pltpu.VMEM(x.shape, x.dtype) for x in operands],
            dma((peers, 3)),
            dma((peers, 3)),
            dma((peers, mates)),
            dma((peers, mates)),
            dma((3,)),
            dma((len(operands),)),
        ],
        compiler_params=pltpu.CompilerParams(
            collective_id=0, has_side_effects=True, vmem_limit_bytes=60 * 1024 * 1024
        ),
    )(*operands)


def sum_kernel(
    sub_count, kern_count, grid_hbm, out, core_out, core_in, far_out, far_in, grid, sems
):
    core_send, core_recv, far_send, far_recv, load_sem = sems
    rows = out.shape[1]
    step = rows // SUM_PARTS
    sub, kern = lax.axis_index("sub"), lax.axis_index("kern")
    cores = [lax.rem(kern + k, kern_count) for k in range(1, kern_count)]
    subs = [lax.rem(sub + s, sub_count) for s in range(1, sub_count)]
    loads = {}
    for s, owner in enumerate(subs + [sub]):
        for k, core in enumerate(cores + [kern]):
            span = pl.ds(pl.multiple_of((owner * kern_count + core) * rows, rows), rows)
            loads[s, k] = pltpu.make_async_copy(
                grid_hbm.at[:, span], grid.at[:, span], load_sem.at[s, k]
            )
            loads[s, k].start()
    barrier = pltpu.get_barrier_semaphore()
    for core in cores:
        pl.semaphore_signal(barrier, inc=1, device_id={"kern": core}, device_id_type=MESH)
    for other in subs:
        pl.semaphore_signal(barrier, inc=1, device_id={"sub": other}, device_id_type=MESH)
    pl.semaphore_wait(barrier, len(cores) + len(subs))

    def rows_of(owner_sub, owner_kern, part):
        start = (owner_sub * kern_count + owner_kern) * rows + part * step
        return pl.ds(pl.multiple_of(start, step), step)

    parts = [(z, p) for z in range(2) for p in range(SUM_PARTS)]
    order = [(s, owner) for s, owner in enumerate(subs)] + [(len(subs), sub)]
    near, far = {}, {}
    for s, owner in order:
        for k in range(len(cores)):
            loads[s, k].wait()
        for z, p in parts:
            for k, core in enumerate(cores):
                spot = (s, k, z, pl.ds(p * step, step))
                core_out[spot] = grid[z, rows_of(owner, core, p)].astype(jnp.bfloat16)
                copy = pltpu.make_async_remote_copy(
                    src_ref=core_out.at[spot],
                    dst_ref=core_in.at[spot],
                    send_sem=core_send.at[s, k, z, p],
                    recv_sem=core_recv.at[s, k, z, p],
                    device_id={"kern": core},
                    device_id_type=MESH,
                )
                copy.start()
                near[s, k, z, p] = copy

    def chip_total(s, owner, z, p):
        total = grid[z, rows_of(owner, kern, p)]
        for k in range(len(cores)):
            near[s, k, z, p].wait_recv()
            total += core_in[s, k, z, pl.ds(p * step, step)].astype(jnp.float32)
        return total

    for s in range(len(order)):
        loads[s, len(cores)].wait()
    for s, owner in order[:-1]:
        for z, p in parts:
            spot = (s, z, pl.ds(p * step, step))
            far_out[spot] = chip_total(s, owner, z, p).astype(jnp.bfloat16)
            copy = pltpu.make_async_remote_copy(
                src_ref=far_out.at[spot],
                dst_ref=far_in.at[spot],
                send_sem=far_send.at[s, z, p],
                recv_sem=far_recv.at[s, z, p],
                device_id={"sub": owner},
                device_id_type=MESH,
            )
            copy.start()
            far[s, z, p] = copy
    for z, p in parts:
        out[z, pl.ds(p * step, step)] = chip_total(len(subs), sub, z, p)
    for z, p in parts:
        for s in range(len(subs)):
            far[s, z, p].wait_recv()
            out[z, pl.ds(p * step, step)] += far_in[s, z, pl.ds(p * step, step)].astype(
                jnp.float32
            )
    for copy in [*near.values(), *far.values()]:
        copy.wait_send()


def sum_rows(grid):
    sub_count, kern_count = lax.axis_size("sub"), lax.axis_size("kern")
    rows = grid.shape[1] // (sub_count * kern_count)
    subs, cores = max(sub_count - 1, 1), max(kern_count - 1, 1)

    def kernel(*refs):
        sum_kernel(sub_count, kern_count, *refs[:7], refs[7:])

    vmem = pl.BlockSpec(memory_space=pltpu.VMEM)
    dma = pltpu.SemaphoreType.DMA
    part = (2, rows, grid.shape[2])
    return pl.pallas_call(
        kernel,
        out_shape=jax.ShapeDtypeStruct(part, jnp.float32),
        in_specs=[pl.BlockSpec(memory_space=pltpu.HBM)],
        out_specs=vmem,
        scratch_shapes=[
            pltpu.VMEM((sub_count, cores) + part, jnp.bfloat16),
            pltpu.VMEM((sub_count, cores) + part, jnp.bfloat16),
            pltpu.VMEM((subs,) + part, jnp.bfloat16),
            pltpu.VMEM((subs,) + part, jnp.bfloat16),
            pltpu.VMEM(grid.shape, jnp.float32),
            dma((sub_count, cores, 2, SUM_PARTS)),
            dma((sub_count, cores, 2, SUM_PARTS)),
            dma((subs, 2, SUM_PARTS)),
            dma((subs, 2, SUM_PARTS)),
            dma((sub_count, kern_count)),
        ],
        compiler_params=pltpu.CompilerParams(
            collective_id=1, has_side_effects=True, vmem_limit_bytes=52 * 1024 * 1024
        ),
    )(grid)


def grid_kernel(
    support,
    blocks,
    meta,
    screens,
    lines,
    rows_hbm,
    cols_hbm,
    grid,
    rows_tab,
    cols_tab,
    table_sem,
    hats,
    line_rows,
    picked,
):
    tables = [
        pltpu.make_async_copy(rows_hbm, rows_tab, table_sem.at[0]),
        pltpu.make_async_copy(cols_hbm, cols_tab, table_sem.at[1]),
    ]
    for table in tables:
        table.start()
    width = 2 * support
    window = support + SUBLANES
    sources = meta.shape[0]
    me = lax.axis_index("band")
    lane = lax.broadcasted_iota(jnp.int32, (support, width), 1)

    def make_hat(s, carry):
        upper = screens[s].astype(jnp.float32)
        turned = pltpu.roll(upper, support, 1)
        lower = jnp.where(lane < support, -turned, turned)
        hats[s, 0:support, :] = upper.astype(jnp.bfloat16)
        hats[s, support:width, :] = lower.astype(jnp.bfloat16)
        return carry

    lax.fori_loop(0, screens.shape[0], make_hat, 0, unroll=8)
    grid[...] = jnp.zeros_like(grid)
    packed = lines[...].astype(jnp.float32)
    real_half = lax.broadcasted_iota(jnp.int32, packed.shape, 1) < support
    line_rows[0] = jnp.where(real_half, packed, 0.0)
    line_rows[1] = jnp.where(real_half, pltpu.roll(packed, support, 1), 0.0)

    def pick_source(source, count):
        for b in range(blocks):
            picked[count] = source * blocks + b
            count = count + (meta[source, 0, b] == me).astype(jnp.int32)
        return count

    count = lax.fori_loop(0, sources, pick_source, jnp.int32(0))
    for k in range(GROUP):
        picked[count + k] = 0
    lane_window = lax.broadcasted_iota(jnp.int32, (window, width), 1)

    for table in tables:
        table.wait()

    def turn(g, carry):
        places, lefts, halves, kernels, patches = [], [], [], [], []
        for k in range(GROUP):
            slot = g * GROUP + k
            i = picked[slot]
            keep = (slot < count).astype(jnp.float32)
            source, b = lax.div(i, blocks), lax.rem(i, blocks)
            screen, row_off, col_off, row, col = (meta[source, f, b] for f in range(1, 6))
            row_at = jnp.minimum(row // SUBLANES, (BR - window) // SUBLANES)
            col_at = jnp.minimum(col // width, NCOL // width - 2)
            row_shift = row - row_at * SUBLANES
            places.append((row_at, col_at, col - col_at * width))
            lefts.append((i, keep, col_off))
            halves.append(
                jnp.dot(
                    rows_tab[row_off * (SUBLANES + 1) + row_shift],
                    hats[screen],
                    preferred_element_type=jnp.float32,
                ).astype(jnp.bfloat16)
            )
        for (i, keep, col_off), half in zip(lefts, halves):
            kernels.append(
                jnp.dot(half, cols_tab[col_off], preferred_element_type=jnp.float32).astype(
                    jnp.bfloat16
                )
            )
        for (i, keep, col_off), kernel in zip(lefts, kernels):
            spread = [
                pltpu.roll(
                    jnp.broadcast_to(
                        line_rows[z, pl.ds(i, 1), :] * keep, (support, width)
                    ),
                    0,
                    1,
                    stride=1,
                    stride_axis=0,
                )
                for z in range(2)
            ]
            toeplitz = jnp.concatenate(
                [
                    jnp.concatenate([spread[0], spread[1]], axis=1),
                    jnp.concatenate([-spread[1], spread[0]], axis=1),
                ],
                axis=0,
            ).astype(jnp.bfloat16)
            patches.append(jnp.dot(kernel, toeplitz, preferred_element_type=jnp.float32))
        for patch, (row_at, col_at, col_shift) in zip(patches, places):
            rows = pl.ds(pl.multiple_of(row_at * SUBLANES, SUBLANES), window)
            left = pl.ds(pl.multiple_of(col_at * width, width), width)
            right = pl.ds(pl.multiple_of(col_at * width + width, width), width)
            for z in range(2):
                turned = pltpu.roll(
                    patch[:window, z * width : (z + 1) * width], lax.rem(col_shift, width), 1
                )
                inside = lane_window >= col_shift
                grid[z, rows, left] += jnp.where(inside, turned, 0.0)
                grid[z, rows, right] += jnp.where(inside, 0.0, turned)
        return carry

    lax.fori_loop(0, (count + GROUP - 1) // GROUP, turn, 0)


def body(
    screens, visibilities, vis_columns, band_route, screen_choice, offsets, row_cell, col_cell
):
    support = screens.shape[-1]
    width = 2 * support
    tables = dft_tables(support)
    patch_rows = -(-(support + SUBLANES) // 16) * 16
    blocks = visibilities.shape[0]
    every_screen, every_line, every_meta = gather(
        screens,
        visibilities,
        vis_columns,
        band_route.T,
        screen_choice[None],
        offsets.T,
        row_cell[None],
        col_cell[None],
    )
    row_table, col_table = row_tables(tables, patch_rows), col_tables(tables)
    hbm = pl.BlockSpec(memory_space=pltpu.HBM)
    vmem = pl.BlockSpec(memory_space=pltpu.VMEM)
    grid_band = pl.pallas_call(
        functools.partial(grid_kernel, support, blocks),
        out_shape=jax.ShapeDtypeStruct((2, BR, NCOL), jnp.float32),
        in_specs=[pl.BlockSpec(memory_space=pltpu.SMEM), vmem, vmem, hbm, hbm],
        out_specs=vmem,
        scratch_shapes=[
            pltpu.VMEM(row_table.shape, jnp.bfloat16),
            pltpu.VMEM(col_table.shape, jnp.bfloat16),
            pltpu.SemaphoreType.DMA((2,)),
            pltpu.VMEM((every_screen.shape[0], width, width), jnp.bfloat16),
            pltpu.VMEM((2,) + every_line.shape, jnp.float32),
            pltpu.SMEM((every_meta.shape[0] * blocks + GROUP,), jnp.int32),
        ],
        compiler_params=pltpu.CompilerParams(vmem_limit_bytes=60 * 1024 * 1024),
    )(every_meta, every_screen, every_line, row_table, col_table)
    return sum_rows(grid_band)


def solution(mesh):
    in_specs = (
        P("band", None, None, None),
        P(("grp", "band", "sub", "kern"), None, None),
        P(("grp", "band", "sub", "kern"), None),
        P(("grp", "band", "sub", "kern"), None),
        P(("grp", "band", "sub", "kern")),
        P(("grp", "band", "sub", "kern"), None),
        P(("grp", "band", "sub", "kern")),
        P(("grp", "band", "sub", "kern")),
    )
    out_specs = P(None, ("grp", "band", "sub", "kern"), None)
    return jax.shard_map(body, mesh=mesh, in_specs=in_specs, out_specs=out_specs, check_vma=False)
```
